128 devices in a mesh: lon: 16 (over x_lo, z, core), lat: 8 (over x_hi, y).
Axes of the slice: x: 4 (x_hi: 2, x_lo: 2; x = x_hi * 2 + x_lo), y: 4, z: 4, core: 2. Of those that a mesh axis runs over, the one named last changes fastest.
Arguments:
- tokens: bfloat16 [384, 768, 512], P('lat', 'lon'), may hold values from -6 to 6
- valid: int32 [384, 768], P('lat', 'lon'), may hold values from 0 to 1, as said below
- w_qkv: bfloat16 [2, 512, 1536], replicated, may hold values from -1.5 to 1.5
- w_out: bfloat16 [2, 512, 512], replicated, may hold values from -0.25 to 0.25
- w_up: bfloat16 [2, 512, 2048], replicated, may hold values from -0.25 to 0.25
- w_down: bfloat16 [2, 2048, 512], replicated, may hold values from -0.125 to 0.125
Outputs:
- result: bfloat16 [384, 768, 512], P('lat', 'lon')
The draws below stay inside these ranges and needn't reach their ends.
Inputs may be any that keep to these rules, and one draw needn't show every extreme that they name: In each band of 12 longitude columns starting at a multiple of 12, valid is 0 on the last p latitude rows of the grid and 1 elsewhere, p from 0 to 5; p = 5 in some band.
All inputs are finite; a program needn't handle non-finite values.
Results may differ from the reference program's by a relative error of at most 0.025.
Values may be sent and summed in bfloat16 or wider, within the bound.
A program may use at most 192 MiB of HBM per device.

```python
import jax
import jax.numpy as jnp
from jax import lax

D = 512
HEADS = 16
FF = 2048
WIN_H = 6
WIN_W = 12
PADR = 5
ROWS = 384
COLS = 768


def draw_valid(key, part):
    key = jax.random.fold_in(key, 5)
    first_key, second_key = jax.random.split(key)
    bands = COLS // WIN_W
    padding = jax.random.randint(first_key, (bands,), 0, PADR + 1)
    chosen = jax.random.randint(second_key, (), 0, bands)
    padding = jnp.where(jnp.arange(bands) == chosen, PADR, padding)
    limit = ROWS - jnp.repeat(padding, WIN_W)
    rows_at = jnp.arange(ROWS)[:, None]
    return (rows_at < limit[None, :]).astype(jnp.int32)


def draw_w_qkv(key, part):
    key = jax.random.fold_in(key, 11)
    base_key = jax.random.fold_in(key, 0)
    base = jax.random.normal(base_key, (2, D, 3 * D), jnp.float32) * D ** (-0.5)
    base = jnp.clip(base, -6.0 * D ** (-0.5), 6.0 * D ** (-0.5))
    return base.astype(jnp.bfloat16)


def levels(rng, shape, pieces, low, high):
    level, own = 1.0, jax.random.fold_in(rng, 6)
    for position, parts in pieces:
        steps = jnp.exp(jax.random.uniform(jax.random.fold_in(own, position), (parts,), jnp.float32, low / len(pieces), high / len(pieces)))
        level = level * jnp.repeat(steps, shape[position] // parts).reshape([-1 if axis == position else 1 for axis in range(len(shape))])
    return level


def normal_values(stream_key, shape, scale, bound, shards=(), kind=jnp.bfloat16):
    entries = scale * jax.random.normal(stream_key, shape, jnp.float32)
    if shards:
        entries = entries * levels(stream_key, shape, shards, -0.22, 0.18)
    return jnp.clip(entries, -bound, bound).astype(kind)


def setup_inputs(seed: int = 0) -> dict:
    key_list = jax.random.split(jax.random.key(seed), 7)
    return {
        "tokens": normal_values(key_list[0], (ROWS, COLS, D), 1.0, 6.0, ((0, 8), (1, 16))),
        "valid": draw_valid(jax.random.fold_in(key_list[6], 71), 0),
        "w_qkv": draw_w_qkv(jax.random.fold_in(key_list[6], 71), 0),
        "w_out": normal_values(key_list[3], (2, D, D), D ** -0.5, 0.25),
        "w_up": normal_values(key_list[4], (2, D, FF), D ** -0.5, 0.25),
        "w_down": normal_values(key_list[5], (2, FF, D), FF ** -0.5, 0.125),
    }


def layer_norm(values):
    wide = values.astype(jnp.float32)
    center = wide - lax.optimization_barrier(jnp.mean(wide, axis=-1, keepdims=True))
    spread = lax.optimization_barrier(jnp.mean(center * center, axis=-1, keepdims=True))
    return center * lax.rsqrt(spread + 1e-05)

def to_windows(grid, win_h, win_w):
    height, width = (grid.shape[0], grid.shape[1])
    rest = grid.shape[2:]
    tiles = grid.reshape((height // win_h, win_h, width // win_w, win_w) + rest)
    tiles = jnp.moveaxis(tiles, 2, 1)
    return tiles.reshape((height // win_h * (width // win_w), win_h * win_w) + rest)

def from_windows(windows, height, width, win_h, win_w):
    rest = windows.shape[2:]
    tiles = windows.reshape((height // win_h, width // win_w, win_h, win_w) + rest)
    tiles = jnp.moveaxis(tiles, 1, 2)
    return tiles.reshape((height, width) + rest)

def attend(windows, keyok, region, w_qkv, w_out, w_up, w_down):
    count, length, width = windows.shape
    head_dim = width // HEADS
    normed = layer_norm(windows).astype(jnp.bfloat16).reshape(count * length, width)
    qkv = jnp.dot(normed, w_qkv, preferred_element_type=jnp.float32).astype(jnp.bfloat16)
    qkv = qkv.reshape(count, length, 3, HEADS, head_dim)
    query = qkv[:, :, 0].astype(jnp.float32)
    keys = qkv[:, :, 1].astype(jnp.float32)
    values = qkv[:, :, 2].astype(jnp.float32)
    scores = jnp.einsum('nqhd,nkhd->nhqk', query, keys) * head_dim ** (-0.5)
    itself = jnp.eye(length, dtype=bool)[None]
    allowed = (keyok[:, None, :] | itself) & (region[:, :, None] == region[:, None, :])
    scores = jnp.where(allowed[:, None], scores, -jnp.inf)
    largest = lax.optimization_barrier(jnp.max(scores, axis=-1, keepdims=True))
    expo = jnp.exp(scores - largest)
    probs = (expo / lax.optimization_barrier(jnp.sum(expo, axis=-1, keepdims=True))).astype(jnp.bfloat16)
    mixed = jnp.einsum('nhqk,nkhd->nqhd', probs.astype(jnp.float32), values)
    mixed = mixed.astype(jnp.bfloat16).reshape(count * length, width)
    flat = windows.reshape(count * length, width).astype(jnp.float32)
    resid = (flat + jnp.dot(mixed, w_out, preferred_element_type=jnp.float32)).astype(jnp.bfloat16)
    normed_two = layer_norm(resid).astype(jnp.bfloat16)
    hidden = jax.nn.gelu(jnp.dot(normed_two, w_up, preferred_element_type=jnp.float32)).astype(jnp.bfloat16)
    output = resid.astype(jnp.float32) + jnp.dot(hidden, w_down, preferred_element_type=jnp.float32)
    return output.astype(jnp.bfloat16).reshape(count, length, width)

def run_grid(grid, keyok, w_qkv, w_out, w_up, w_down):
    height, width, feats = grid.shape
    bands = grid.reshape(height // WIN_H, WIN_H, width, feats)
    ok_bands = keyok.reshape(height // WIN_H, WIN_H, width)

    def one_band(pair):
        band, ok_band = pair
        windows = to_windows(band, WIN_H, WIN_W)
        flags = to_windows(ok_band, WIN_H, WIN_W)
        region = jnp.zeros(flags.shape, jnp.int32)
        output = attend(windows, flags, region, w_qkv, w_out, w_up, w_down)
        return from_windows(output, WIN_H, width, WIN_H, WIN_W)
    done = lax.map(one_band, (bands, ok_bands))
    return done.reshape(height, width, feats)

def reference(tokens, valid, w_qkv, w_out, w_up, w_down):
    height = tokens.shape[0]
    half_h = WIN_H // 2
    half_w = WIN_W // 2
    keyok = valid == 1
    first = run_grid(tokens, keyok, w_qkv[0], w_out[0], w_up[0], w_down[0])
    shifted = jnp.pad(first, ((half_h, half_h), (0, 0), (0, 0)))
    shifted = jnp.roll(shifted, -half_w, axis=1)
    ok_shift = jnp.pad(keyok, ((half_h, half_h), (0, 0)))
    ok_shift = jnp.roll(ok_shift, -half_w, axis=1)
    second = run_grid(shifted, ok_shift, w_qkv[1], w_out[1], w_up[1], w_down[1])
    second = jnp.roll(second, half_w, axis=1)[half_h:half_h + height]
    return (second.astype(jnp.float32) * valid.astype(jnp.float32)[:, :, None]).astype(jnp.bfloat16)
```

```python
import jax
import jax.numpy as jnp
import numpy as np
from jax import lax
from jax.experimental import pallas as pl
from jax.experimental.pallas import tpu as pltpu
from jax.sharding import PartitionSpec as P

HEADS = 16
WIN_H = 6
WIN_W = 12
TOK = WIN_H * WIN_W
PAD = 80
EXT = 64
HALO = 16
MESH = pl.DeviceIdType.MESH
BF = jnp.bfloat16
F32 = jnp.float32


def to_window_order(rows, cols, offset, win_h):
    take = np.zeros((rows * 48, rows * cols), np.float32)
    t = 0
    for band in range(rows // win_h):
        for j in range(4):
            for r in range(win_h):
                for c in range(WIN_W):
                    take[t, (band * win_h + r) * cols + offset + j * WIN_W + c] = 1
                    t += 1
    return take


def head_sets():
    head = np.arange(256) // 32
    return np.stack([head // 3 == i for i in range(3)] + [head % 3 == j for j in range(3)])[:, None, :]


def layer_norm(wide):
    center = wide - jnp.mean(wide, axis=-1, keepdims=True)
    spread = jnp.mean(center * center, axis=-1, keepdims=True)
    return (center * lax.rsqrt(spread + 1e-05)).astype(BF)


def gelu(x):
    half = 0.5 * x
    return half + half * jnp.tanh(x * (0.7978845608028654 + 0.035677408136300125 * (x * x)))


def half_heads(q, k, v, sets, allow):
    by_key = jnp.concatenate([k * sets[i] for i in range(3)], 0)
    by_query = jnp.concatenate([q * sets[3 + j] for j in range(3)], 0)
    scores = lax.dot_general(by_key, by_query, (((1,), (1,)), ((), ())), preferred_element_type=F32)
    parts = []
    for i in range(3):
        part = scores[PAD * i : PAD * i + TOK]
        if allow is not None:
            part = jnp.where(allow, part, -jnp.inf)
        largest = jnp.max(part, axis=0, keepdims=True)
        expo = jnp.exp2((part - largest) * (1.4426950408889634 * 32**-0.5))
        total = jnp.sum(expo, axis=0, keepdims=True)
        parts += [expo * (1.0 / total), jnp.zeros((PAD - TOK, 3 * PAD), F32)]
    probs = jnp.concatenate(parts, 0).astype(BF)
    by_value = jnp.concatenate([v * sets[i] for i in range(3)], 0)
    mixed = lax.dot_general(probs, by_value, (((0,), (0,)), ((), ())), preferred_element_type=F32)
    pick = [sets[3 + j].astype(F32) for j in range(3)]
    return (
        mixed[:TOK] * pick[0] + mixed[PAD : PAD + TOK] * pick[1] + mixed[2 * PAD : 2 * PAD + TOK] * pick[2]
    )


def attention(qkv, mixed, sets_ref, count, flags=None, halves=False):
    sets = [sets_ref[i] for i in range(6)]
    key = lax.broadcasted_iota(jnp.int32, (TOK, 3 * PAD), 0)
    lane = lax.broadcasted_iota(jnp.int32, (TOK, 3 * PAD), 1)
    query = lane - PAD * (lane >= PAD).astype(jnp.int32) - PAD * (lane >= 2 * PAD).astype(jnp.int32)
    for pair in range(count // 2):
        for g in range(2):
            both = []
            for w in (2 * pair, 2 * pair + 1):
                allow = None
                if flags is not None:
                    allow = flags[w][:, 0:1] > 0.5
                    if halves:
                        allow = allow & ((key < TOK // 2) == (query < TOK // 2))
                    allow = allow | (key == query)
                q = qkv[w, :, 256 * g : 256 * g + 256]
                k = qkv[w, :, 512 + 256 * g : 768 + 256 * g]
                v = qkv[w, :, 1024 + 256 * g : 1280 + 256 * g]
                both.append(half_heads(q, k, v, sets, allow))
            mixed[2 * TOK * pair : 2 * TOK * pair + 2 * TOK, 256 * g : 256 * g + 256] = jnp.concatenate(
                both, 0
            ).astype(BF)


def window_flags(valid_rows, rows, first_col):
    t = lax.broadcasted_iota(jnp.int32, (TOK, 128), 0)
    lane = lax.broadcasted_iota(jnp.int32, (TOK, 128), 1)
    count = len(rows)
    tall = jnp.zeros((TOK, 128), F32)
    at = lane - first_col
    for half in range(TOK // (count * WIN_W)):
        for r, row in enumerate(rows):
            low = (half * count + r) * WIN_W
            here = (t >= low) & (t < low + WIN_W) & (at == t - low + half * WIN_W)
            tall = jnp.where(here, row, tall)
    return jnp.broadcast_to(jnp.sum(tall, axis=1, keepdims=True), (TOK, 128))


def kernel(
    tok_hbm, valid_ref, wqkv_hbm, wout_hbm, wup_hbm, wdown_hbm, p0, p1, p1t, pp, ppt, sets,
    out_ref,
    tok, ext, yext, ret, vhalo, wqkv, wout, wup, wdown, qkv, mixed, wide, hidden, flags,
    tok_sem, w_sem, halo_s, halo_r, row_s, row_r, diag_s, diag_r, v_s, v_r,
    ret_s, ret_r, corner_s, corner_r, below_s, below_r,
):
    lat, lon = lax.axis_index("lat"), lax.axis_index("lon")
    lats, lons = lax.axis_size("lat"), lax.axis_size("lon")
    north, south = lat == 0, lat == lats - 1
    left, right = lax.rem(lon + lons - 1, lons), lax.rem(lon + 1, lons)

    def tok_copy(p):
        return pltpu.make_async_copy(tok_hbm.at[pl.ds(12 * p, 12)], tok.at[pl.ds(12 * p, 12)], tok_sem.at[p])

    weights = [
        [
            pltpu.make_async_copy(src.at[b], dst.at[b], w_sem.at[b, n])
            for n, (src, dst) in enumerate(
                ((wqkv_hbm, wqkv), (wout_hbm, wout), (wup_hbm, wup), (wdown_hbm, wdown))
            )
        ]
        for b in range(2)
    ]
    tok_copy(3).start()
    weights[0][0].start()
    weights[0][1].start()
    weights[0][2].start()
    weights[0][3].start()
    for p in range(3):
        tok_copy(p).start()
    for n in range(4):
        weights[1][n].start()

    up, down = lax.rem(lat + lats - 1, lats), lax.rem(lat + 1, lats)
    barrier = pltpu.get_barrier_semaphore()
    for partner in ((lat, left), (lat, right), (up, lon), (up, right), (down, lon), (down, left)):
        pl.semaphore_signal(barrier, inc=1, device_id={"lat": partner[0], "lon": partner[1]}, device_id_type=MESH)

    qkv[:, TOK:PAD, :] = jnp.zeros((8, PAD - TOK, 1536), BF)

    @pl.when(north)
    def _():
        ext[0:3] = jnp.zeros((3, EXT, 512), BF)

    def send(src, dst, ssem, rsem, target):
        place = {"lat": target[0], "lon": target[1]}
        return pltpu.make_async_remote_copy(
            src_ref=src, dst_ref=dst, send_sem=ssem, recv_sem=rsem, device_id=place, device_id_type=MESH
        )

    v_copy = send(valid_ref.at[pl.ds(40, 8)], vhalo, v_s, v_r, (lat, left))

    def halo_copy(p):
        rows = pl.ds(3 + 12 * p, 12)
        return send(
            ext.at[rows, pl.ds(0, HALO)], ext.at[rows, pl.ds(48, HALO)], halo_s.at[p], halo_r.at[p], (lat, left)
        )

    row_copy = send(
        ext.at[pl.ds(48, 3), pl.ds(0, 48)], ext.at[pl.ds(0, 3), pl.ds(0, 48)], row_s, row_r, (lat + 1, lon)
    )
    diag_copy = send(
        ext.at[pl.ds(48, 3), pl.ds(0, HALO)], ext.at[pl.ds(0, 3), pl.ds(48, HALO)], diag_s, diag_r, (lat + 1, left)
    )

    def ret_copy(p, low, size):
        rows = pl.ds(low, size)
        return send(yext.at[rows, pl.ds(48, HALO)], ret.at[rows], ret_s.at[p], ret_r.at[p], (lat, right))

    below_copy = send(
        yext.at[pl.ds(0, 3), pl.ds(0, 48)], yext.at[pl.ds(48, 3), pl.ds(0, 48)], below_s, below_r, (lat - 1, lon)
    )
    corner_copy = send(
        yext.at[pl.ds(0, 3), pl.ds(48, HALO)], ret.at[pl.ds(48, 3)], corner_s, corner_r, (lat - 1, right)
    )
    pole_copy = send(
        yext.at[pl.ds(48, 3), pl.ds(48, HALO)], ret.at[pl.ds(48, 3)], corner_s, corner_r, (lat, right)
    )

    def project(b, x, tokens):
        width = tokens // TOK
        wide[0:tokens] = x
        out = jnp.dot(layer_norm(x), wqkv[b], preferred_element_type=F32)
        for w in range(width):
            qkv[w, 0:TOK, :] = out[TOK * w : TOK * w + TOK].astype(BF)

    def feed(b, tokens):
        resid = wide[0:tokens] + jnp.dot(mixed[0:tokens], wout[b], preferred_element_type=F32)
        resid = resid.astype(BF)
        normed = layer_norm(resid.astype(F32))
        for n in range(4):
            cut = slice(512 * n, 512 * n + 512)
            hidden[0:tokens, cut] = gelu(jnp.dot(normed, wup[b, :, cut], preferred_element_type=F32)).astype(BF)
        down = jnp.dot(hidden[0:tokens], wdown[b], preferred_element_type=F32)
        return (resid.astype(F32) + down).astype(BF)

    weights[0][0].wait()

    def block0(step, carry):
        p = lax.rem(step + 3, 4)
        tok_copy(p).wait()
        for band in range(2):
            x = tok[pl.ds(12 * p + 6 * band, 6)].reshape(288, 512)
            wide[288 * band : 288 * band + 288] = jnp.dot(p0[...], x, preferred_element_type=F32)
        project(0, wide[...], 576)
        masked = south & (p == 3)

        @pl.when(~masked)
        def _():
            attention(qkv, mixed, sets, 8)

        @pl.when(masked)
        def _():
            rows = [valid_wide(r) for r in range(2, 8)]
            for w in range(4):
                flags[w] = jnp.ones((TOK, 128), F32)
                flags[4 + w] = window_flags(None, rows, 12 * w)
            attention(qkv, mixed, sets, 8, flags)

        @pl.when(step == 0)
        def _():
            for n in range(1, 4):
                weights[0][n].wait()

        y = feed(0, 576)
        for band in range(2):
            nat = lax.dot_general(
                p0[...], y[288 * band : 288 * band + 288], (((0,), (0,)), ((), ())), preferred_element_type=F32
            )
            ext[pl.ds(3 + 12 * p + 6 * band, 6), 0:48] = nat.astype(BF).reshape(6, 48, 512)

        @pl.when(step == 0)
        def _():
            v_copy.start()

            @pl.when(~south)
            def _():
                row_copy.start()
                diag_copy.start()

        halo_copy(p).start()
        return carry

    def valid_wide(r):
        return vflag[r : r + 1, :]

    vflag = vhalo_flags(valid_ref, None)
    pl.semaphore_wait(barrier, 6)
    lax.fori_loop(0, 4, block0, 0)

    for n in range(4):
        weights[1][n].wait()
    v_copy.wait()
    vflag1 = vhalo_flags(valid_ref, vhalo)

    def block1(p, carry):
        @pl.when((p == 0) & ~north)
        def _():
            row_copy.wait_recv()
            diag_copy.wait_recv()

        halo_copy(p).wait_recv()
        for band in range(2):
            x = ext[pl.ds(12 * p + 6 * band, 6)].reshape(6 * EXT, 512)
            wide[288 * band : 288 * band + 288] = jnp.dot(p1[...], x, preferred_element_type=F32)
        project(1, wide[...], 576)
        masked = (south & (p == 3)) | (north & (p == 0))

        @pl.when(~masked)
        def _():
            attention(qkv, mixed, sets, 8)

        @pl.when(masked)
        def _():
            one = jnp.ones((1, 128), F32)
            top = one * jnp.where(north & (p == 0), 0.0, 1.0)
            tail = [jnp.where(p == 3, vflag1[r : r + 1, :], 1.0) for r in range(5)]
            for w in range(4):
                flags[w] = window_flags(None, [top] * 3 + [one] * 3, 6 + 12 * w)
                flags[4 + w] = window_flags(None, [one] + tail, 6 + 12 * w)
            attention(qkv, mixed, sets, 8, flags)

        y = feed(1, 576)
        for band in range(2):
            nat = jnp.dot(p1t[...], y[288 * band : 288 * band + 288], preferred_element_type=F32)
            yext[pl.ds(12 * p + 6 * band, 6)] = nat.astype(BF).reshape(6, EXT, 512)

        @pl.when(p == 0)
        def _():
            ret_copy(0, 3, 9).start()

            @pl.when(~north)
            def _():
                below_copy.start()
                corner_copy.start()

        @pl.when(p > 0)
        def _():
            ret_copy(p, 12 * p, 12).start()

        return carry

    lax.fori_loop(0, 4, block1, 0)

    @pl.when(south)
    def _():
        x = ext[48:51].reshape(3 * EXT, 512)
        wide[0:144] = jnp.dot(pp[...], x, preferred_element_type=F32)
        project(1, wide[0:144], 144)
        for w in range(2):
            flags[w] = window_flags(None, [vflag1[r : r + 1, :] for r in range(5, 8)], 6 + 24 * w)
        attention(qkv, mixed, sets, 2, flags, halves=True)
        y = feed(1, 144)
        nat = jnp.dot(ppt[...], y, preferred_element_type=F32)
        yext[48:51] = nat.astype(BF).reshape(3, EXT, 512)
        pole_copy.start()
        pole_copy.wait()

    @pl.when(~south)
    def _():
        below_copy.wait_recv()
        corner_copy.wait_recv()

    ret_copy(0, 3, 9).wait_recv()
    for p in range(1, 4):
        ret_copy(p, 12 * p, 12).wait_recv()
    col = lax.broadcasted_iota(jnp.int32, (1, HALO, 512), 1)

    def merge(p, carry):
        rows = pl.ds(3 + 8 * p, 8)
        here = pl.ds(8 * p, 8)
        out_ref[here, HALO:48] = yext[rows, HALO:48]
        out_ref[here, 0:HALO] = jnp.where(
            col < 6, ret[rows].astype(F32), yext[rows, 0:HALO].astype(F32)
        ).astype(BF)
        return carry

    lax.fori_loop(0, 6, merge, 0)
    lane = lax.broadcasted_iota(jnp.int32, (48, 128), 1)
    sub = lax.broadcasted_iota(jnp.int32, (48, 128), 0)
    for r in range(8):
        keep = jnp.sum(jnp.where(lane == sub, vflag1[r : r + 1, :], 0.0), axis=1, keepdims=True)
        out_ref[40 + r] = (out_ref[40 + r].astype(F32) * keep).astype(BF)

    for p in range(4):
        halo_copy(p).wait_send()
    ret_copy(0, 3, 9).wait_send()
    for p in range(1, 4):
        ret_copy(p, 12 * p, 12).wait_send()

    @pl.when(~south)
    def _():
        row_copy.wait_send()
        diag_copy.wait_send()

    @pl.when(~north)
    def _():
        below_copy.wait_send()
        corner_copy.wait_send()


def vhalo_flags(valid_ref, vhalo):
    own = valid_ref[40:48, :].astype(F32)
    parts = [own]
    if vhalo is not None:
        parts.append(vhalo[:, 0:HALO].astype(F32))
        parts.append(jnp.zeros((8, 64), F32))
    else:
        parts.append(jnp.zeros((8, 80), F32))
    return jnp.concatenate(parts, axis=1)


def shards(tokens, valid, w_qkv, w_out, w_up, w_down):
    vmem = pl.BlockSpec(memory_space=pltpu.VMEM)
    hbm = pl.BlockSpec(memory_space=pl.ANY)
    dma = pltpu.SemaphoreType.DMA
    take0 = to_window_order(6, 48, 0, 6)
    take1 = to_window_order(6, EXT, 6, 6)
    take_pole = to_window_order(3, EXT, 6, 3)
    constants = [jnp.asarray(a, BF) for a in (take0, take1, take1.T, take_pole, take_pole.T, head_sets())]
    return pl.pallas_call(
        kernel,
        out_shape=jax.ShapeDtypeStruct((48, 48, 512), BF),
        in_specs=[hbm, vmem] + [hbm] * 4 + [vmem] * 6,
        out_specs=vmem,
        scratch_shapes=[
            pltpu.VMEM((48, 48, 512), BF),
            pltpu.VMEM((51, EXT, 512), BF),
            pltpu.VMEM((51, EXT, 512), BF),
            pltpu.VMEM((51, HALO, 512), BF),
            pltpu.VMEM((8, 48), jnp.int32),
            pltpu.VMEM((2, 512, 1536), BF),
            pltpu.VMEM((2, 512, 512), BF),
            pltpu.VMEM((2, 512, 2048), BF),
            pltpu.VMEM((2, 2048, 512), BF),
            pltpu.VMEM((8, PAD, 1536), BF),
            pltpu.VMEM((576, 512), BF),
            pltpu.VMEM((576, 512), F32),
            pltpu.VMEM((576, 2048), BF),
            pltpu.VMEM((8, TOK, 128), F32),
            dma((4,)), dma((2, 4)), dma((4,)), dma((4,)), dma(()), dma(()), dma(()), dma(()), dma(()), dma(()),
            dma((4,)), dma((4,)), dma(()), dma(()), dma(()), dma(()),
        ],
        compiler_params=pltpu.CompilerParams(
            collective_id=0, has_side_effects=True, vmem_limit_bytes=60 << 20
        ),
        name="swin",
    )(tokens, valid, w_qkv, w_out, w_up, w_down, *constants)


def solution(mesh):
    return jax.shard_map(
        shards,
        mesh=mesh,
        in_specs=(P("lat", "lon", None), P("lat", "lon"), P(), P(), P(), P()),
        out_specs=P("lat", "lon", None),
        check_vma=False,
    )
```

```python
import jax
import jax.numpy as jnp
import numpy as np
from jax import lax
from jax.experimental import pallas as pl
from jax.experimental.pallas import tpu as pltpu
from jax.sharding import PartitionSpec as P

HEADS = 16
WIN_H = 6
WIN_W = 12
TOK = WIN_H * WIN_W
PAD = 80
EXT = 64
HALO = 16
MESH = pl.DeviceIdType.MESH
BF = jnp.bfloat16
F32 = jnp.float32


ORDER = [(0, 3), (1, 3), (0, 0), (0, 1), (0, 2), (1, 0), (1, 1), (1, 2)]


def head_sets():
    head = np.arange(256) // 32
    return np.stack([head // 3 == i for i in range(3)] + [head % 3 == j for j in range(3)])[:, None, :]


def layer_norm(wide):
    center = wide - jnp.mean(wide, axis=-1, keepdims=True)
    spread = jnp.mean(center * center, axis=-1, keepdims=True)
    return (center * lax.rsqrt(spread + 1e-05)).astype(BF)


def gelu(x):
    half = 0.5 * x
    return half + half * jnp.tanh(x * (0.7978845608028654 + 0.035677408136300125 * (x * x)))


def half_heads(q, k, v, sets, bias):
    by_key = jnp.concatenate([k * sets[i] for i in range(3)], 0)
    by_query = jnp.concatenate([q * sets[3 + j] for j in range(3)], 0)
    scores = lax.dot_general(by_key, by_query, (((1,), (1,)), ((), ())), preferred_element_type=F32)
    parts = []
    for i in range(3):
        part = scores[PAD * i : PAD * i + TOK] + bias
        largest = jnp.max(part, axis=0, keepdims=True)
        expo = jnp.exp2((part - largest) * (1.4426950408889634 * 32**-0.5))
        total = jnp.sum(expo, axis=0, keepdims=True)
        parts += [expo * (1.0 / total), jnp.zeros((PAD - TOK, 3 * PAD), F32)]
    probs = jnp.concatenate(parts, 0).astype(BF)
    by_value = jnp.concatenate([v * sets[i] for i in range(3)], 0)
    mixed = lax.dot_general(probs, by_value, (((0,), (0,)), ((), ())), preferred_element_type=F32)
    pick = [sets[3 + j].astype(F32) for j in range(3)]
    return (
        mixed[:TOK] * pick[0] + mixed[PAD : PAD + TOK] * pick[1] + mixed[2 * PAD : 2 * PAD + TOK] * pick[2]
    )


def window_bias(rows, first_col, halves=False):
    t = lax.broadcasted_iota(jnp.int32, (TOK, 128), 0)
    lane = lax.broadcasted_iota(jnp.int32, (TOK, 128), 1)
    tall = jnp.zeros((TOK, 128), F32)
    at = lane - first_col
    for half in range(2 if halves else 1):
        for r, row in enumerate(rows):
            low = (half * len(rows) + r) * WIN_W
            here = (t >= low) & (t < low + WIN_W) & (at == t - low + half * WIN_W)
            tall = jnp.where(here, row, tall)
    flag = jnp.sum(tall, axis=1, keepdims=True)
    key = lax.broadcasted_iota(jnp.int32, (TOK, 256), 0)
    query = lax.broadcasted_iota(jnp.int32, (TOK, 256), 1)
    query = query - PAD * ((query >= PAD).astype(jnp.int32) + (query >= 2 * PAD).astype(jnp.int32))
    allow = flag > 0.5
    if halves:
        allow = allow & ((key < TOK // 2) == (query < TOK // 2))
    allow = allow | (key == query) | (query >= TOK)
    return jnp.where(allow, 0.0, -jnp.inf)


def kernel(
    tok_hbm, valid_ref, wqkv_hbm, wout_hbm, wup_hbm, wdown_hbm, sets_ref,
    out_hbm,
    tok, ext, yext, ret, vhalo, wqkv, wout, wup, wdown, qkv, mixed, wide, resid, hidden, bias,
    tok_sem, w_sem, out_sem, halo_s, halo_r, row_s, row_r, diag_s, diag_r, v_s, v_r,
    ret_s, ret_r, corner_s, corner_r, below_s, below_r,
):
    lat, lon = lax.axis_index("lat"), lax.axis_index("lon")
    lats, lons = lax.axis_size("lat"), lax.axis_size("lon")
    north, south = lat == 0, lat == lats - 1
    left, right = lax.rem(lon + lons - 1, lons), lax.rem(lon + 1, lons)

    def tok_copy(p):
        return pltpu.make_async_copy(tok_hbm.at[pl.ds(12 * p, 12)], tok.at[pl.ds(12 * p, 12)], tok_sem.at[p])

    weights = [
        [
            pltpu.make_async_copy(src.at[b], dst.at[b], w_sem.at[b, n])
            for n, (src, dst) in enumerate(
                ((wqkv_hbm, wqkv), (wout_hbm, wout), (wup_hbm, wup), (wdown_hbm, wdown))
            )
        ]
        for b in range(2)
    ]
    tok_copy(3).start()
    for n in range(4):
        weights[0][n].start()
    for p in range(3):
        tok_copy(p).start()
    for n in range(4):
        weights[1][n].start()

    up, down = lax.rem(lat + lats - 1, lats), lax.rem(lat + 1, lats)
    barrier = pltpu.get_barrier_semaphore()
    for partner in ((lat, left), (lat, right), (up, lon), (up, right), (down, lon), (down, left)):
        place = {"lat": partner[0], "lon": partner[1]}
        pl.semaphore_signal(barrier, inc=1, device_id=place, device_id_type=MESH)

    qkv[:, TOK:PAD, :] = jnp.zeros((8, PAD - TOK, 1536), BF)
    bias[...] = jnp.zeros((8, TOK, 256), F32)

    @pl.when(north)
    def _():
        ext[0:3] = jnp.zeros((3, EXT, 512), BF)

    def send(src, dst, ssem, rsem, target):
        place = {"lat": target[0], "lon": target[1]}
        return pltpu.make_async_remote_copy(
            src_ref=src, dst_ref=dst, send_sem=ssem, recv_sem=rsem, device_id=place, device_id_type=MESH
        )

    v_copy = send(valid_ref.at[pl.ds(40, 8)], vhalo, v_s, v_r, (lat, left))

    def halo_copy(p):
        rows = pl.ds(3 + 12 * p, 12)
        return send(
            ext.at[rows, pl.ds(0, HALO)], ext.at[rows, pl.ds(48, HALO)], halo_s.at[p], halo_r.at[p], (lat, left)
        )

    row_copy = send(
        ext.at[pl.ds(48, 3), pl.ds(0, 48)], ext.at[pl.ds(0, 3), pl.ds(0, 48)], row_s, row_r, (lat + 1, lon)
    )
    diag_copy = send(
        ext.at[pl.ds(48, 3), pl.ds(0, HALO)], ext.at[pl.ds(0, 3), pl.ds(48, HALO)], diag_s, diag_r, (lat + 1, left)
    )

    def ret_copy(p, low, size):
        rows = pl.ds(low, size)
        return send(yext.at[rows, pl.ds(48, HALO)], ret.at[rows], ret_s.at[p], ret_r.at[p], (lat, right))

    below_copy = send(
        yext.at[pl.ds(0, 3), pl.ds(0, 48)], yext.at[pl.ds(48, 3), pl.ds(0, 48)], below_s, below_r, (lat - 1, lon)
    )
    corner_copy = send(
        yext.at[pl.ds(0, 3), pl.ds(48, HALO)], ret.at[pl.ds(48, 3)], corner_s, corner_r, (lat - 1, right)
    )
    pole_copy = send(
        yext.at[pl.ds(48, 3), pl.ds(48, HALO)], ret.at[pl.ds(48, 3)], corner_s, corner_r, (lat, right)
    )

    def out_copy(n, low, size):
        return pltpu.make_async_copy(
            yext.at[pl.ds(low, size), pl.ds(0, 48)], out_hbm.at[pl.ds(low - 3, size)], out_sem.at[n]
        )

    sets = [sets_ref[i] for i in range(6)]

    def gather0(p):
        x = tok[pl.ds(12 * p, 12)].astype(F32)
        for w, (band, j) in enumerate(ORDER):
            wide[TOK * w : TOK * w + TOK] = jnp.concatenate(
                [x[6 * band + r, 12 * j : 12 * j + 12] for r in range(6)], 0
            )

    def gather1(p):
        x = ext[pl.ds(12 * p, 12)].astype(F32)
        for w, (band, j) in enumerate(ORDER):
            wide[TOK * w : TOK * w + TOK] = jnp.concatenate(
                [x[6 * band + r, 12 * j + 6 : 12 * j + 18] for r in range(6)], 0
            )

    def project(b, tokens):
        out = jnp.dot(layer_norm(wide[0:tokens]), wqkv[b], preferred_element_type=F32)
        for w in range(tokens // TOK):
            qkv[w, 0:TOK, :] = out[TOK * w : TOK * w + TOK].astype(BF)

    def attend(pair):
        for g in range(2):
            both = []
            for w in (2 * pair, 2 * pair + 1):
                q = qkv[w, :, 256 * g : 256 * g + 256]
                k = qkv[w, :, 512 + 256 * g : 768 + 256 * g]
                v = qkv[w, :, 1024 + 256 * g : 1280 + 256 * g]
                both.append(half_heads(q, k, v, sets, bias[w, :, 0 : 3 * PAD]))
            mixed[2 * TOK * pair : 2 * TOK * pair + 2 * TOK, 256 * g : 256 * g + 256] = jnp.concatenate(
                both, 0
            ).astype(BF)

    def add_mixed(b, rows):
        total = wide[rows] + jnp.dot(mixed[rows], wout[b], preferred_element_type=F32)
        total = total.astype(BF)
        resid[rows] = total
        return layer_norm(total.astype(F32))

    def expand(b, normed, rows, n):
        cut = slice(512 * n, 512 * n + 512)
        hidden[rows, cut] = gelu(jnp.dot(normed, wup[b, :, cut], preferred_element_type=F32)).astype(BF)

    def contract(b, rows):
        return resid[rows].astype(F32) + jnp.dot(hidden[rows], wdown[b], preferred_element_type=F32)

    def scatter0(y, p):
        rows = [
            y[TOK * w + 12 * r : TOK * w + 12 * r + 12]
            for band in range(2)
            for r in range(6)
            for w in (ORDER.index((band, j)) for j in range(4))
        ]
        ext[pl.ds(3 + 12 * p, 12), 0:48] = jnp.concatenate(rows, 0).astype(BF).reshape(12, 48, 512)

    def scatter1(y, p):
        for band in range(2):
            for r in range(6):
                row = [y[TOK * w + 12 * r : TOK * w + 12 * r + 12] for w in (ORDER.index((band, j)) for j in range(4))]
                row = [jnp.zeros((6, 512), F32)] + row + [jnp.zeros((10, 512), F32)]
                yext[12 * p + 6 * band + r] = jnp.concatenate(row, 0).astype(BF)

    everything = slice(0, 576)

    def step(b_feed, p_feed, b_att, gather, p_att, scatter):
        normed = add_mixed(b_feed, everything)
        gather(p_att)
        project(b_att, 576)
        for n in range(4):
            expand(b_feed, normed, everything, n)
            attend(n)
        scatter(contract(b_feed, everything), p_feed)

    vflag = flag_rows(valid_ref, None)

    @pl.when(south)
    def _():
        for w, (band, j) in enumerate(ORDER):
            if band == 1:
                bias[w] = window_bias([vflag[r : r + 1] for r in range(2, 8)], 12 * j)

    tok_copy(3).wait()
    weights[0][0].wait()
    gather0(3)
    project(0, 576)
    for n in range(4):
        attend(n)

    @pl.when(south)
    def _():
        for w, (band, j) in enumerate(ORDER):
            if band == 1:
                bias[w] = jnp.zeros((TOK, 256), F32)

    for n in range(1, 4):
        weights[0][n].wait()
    pl.semaphore_wait(barrier, 6)
    v_copy.start()

    def block0(p, carry):
        tok_copy(p).wait()
        before = lax.rem(p + 3, 4)
        step(0, before, 0, gather0, p, scatter0)

        @pl.when((p == 0) & ~south)
        def _():
            row_copy.start()
            diag_copy.start()

        halo_copy(before).start()
        return carry

    lax.fori_loop(0, 3, block0, 0)

    v_copy.wait()
    vflag = flag_rows(valid_ref, vhalo)
    one = jnp.ones((1, 128), F32)
    for n in range(4):
        weights[1][n].wait()

    @pl.when(north)
    def _():
        for w, (band, j) in enumerate(ORDER):
            if band == 0:
                bias[w] = window_bias([0.0 * one] * 3 + [one] * 3, 6 + 12 * j)

    @pl.when(~north)
    def _():
        row_copy.wait_recv()
        diag_copy.wait_recv()

    halo_copy(3).wait_recv()
    halo_copy(0).wait_recv()
    step(0, 2, 1, gather1, 0, scatter0)
    halo_copy(2).start()

    @pl.when(north)
    def _():
        for w, (band, j) in enumerate(ORDER):
            if band == 0:
                bias[w] = jnp.zeros((TOK, 256), F32)

    def merge(low, size):
        rows = pl.ds(low, size)
        col = lax.broadcasted_iota(jnp.int32, (1, HALO, 512), 1)
        yext[rows, 0:HALO] = jnp.where(
            col < 6, ret[rows].astype(F32), yext[rows, 0:HALO].astype(F32)
        ).astype(BF)

    def block1(p, carry):
        @pl.when(p < 3)
        def _():
            halo_copy(p).wait_recv()

        @pl.when(south & (p == 3))
        def _():
            for w, (band, j) in enumerate(ORDER):
                if band == 1:
                    bias[w] = window_bias([one] + [vflag[r : r + 1] for r in range(5)], 6 + 12 * j)

        step(1, p - 1, 1, gather1, p, scatter1)

        @pl.when(p == 1)
        def _():
            ret_copy(0, 3, 9).start()

            @pl.when(~north)
            def _():
                below_copy.start()
                corner_copy.start()

        @pl.when(p == 2)
        def _():
            ret_copy(1, 12, 12).start()
            ret_copy(0, 3, 9).wait_recv()
            merge(3, 9)
            out_copy(0, 3, 9).start()

        @pl.when(p == 3)
        def _():
            ret_copy(2, 24, 12).start()
            ret_copy(1, 12, 12).wait_recv()
            merge(12, 12)
            out_copy(1, 12, 12).start()

        return carry

    lax.fori_loop(1, 4, block1, 0)

    first, others = slice(0, 2 * TOK), slice(2 * TOK, 8 * TOK)
    normed = add_mixed(1, first)
    for n in range(4):
        expand(1, normed, first, n)
    y = contract(1, first)
    for band in range(2):
        for r in range(6):
            row = [y[TOK * band + 12 * r + 6 : TOK * band + 12 * r + 12], jnp.zeros((10, 512), F32)]
            yext[36 + 6 * band + r, 48:64] = jnp.concatenate(row, 0).astype(BF)
    ret_copy(3, 36, 12).start()
    normed = add_mixed(1, others)
    for n in range(4):
        expand(1, normed, others, n)
    y = jnp.concatenate([y, contract(1, others)], 0)
    for band in range(2):
        for r in range(6):
            row = [y[TOK * w + 12 * r : TOK * w + 12 * r + 12] for w in (ORDER.index((band, j)) for j in range(4))]
            row = [jnp.zeros((6, 512), F32)] + row
            yext[36 + 6 * band + r, 0:48] = jnp.concatenate(row, 0)[0:48].astype(BF)

    @pl.when(south)
    def _():
        x = ext[48:51].astype(F32)
        for w in range(2):
            wide[TOK * w : TOK * w + TOK] = jnp.concatenate(
                [x[r, 12 * j + 6 : 12 * j + 18] for j in (2 * w, 2 * w + 1) for r in range(3)], 0
            )
            bias[w] = window_bias([vflag[r : r + 1] for r in range(5, 8)], 6 + 24 * w, halves=True)
        project(1, 2 * TOK)
        attend(0)
        normed = add_mixed(1, first)
        for n in range(4):
            expand(1, normed, first, n)
        y = contract(1, first)
        for r in range(3):
            row = [y[36 * j + 12 * r : 36 * j + 12 * r + 12] for j in range(4)]
            row = [jnp.zeros((6, 512), F32)] + row + [jnp.zeros((10, 512), F32)]
            yext[48 + r] = jnp.concatenate(row, 0).astype(BF)
        pole_copy.start()
        pole_copy.wait()

    @pl.when(~south)
    def _():
        below_copy.wait_recv()
        corner_copy.wait_recv()

    ret_copy(2, 24, 12).wait_recv()
    merge(24, 12)
    out_copy(2, 24, 12).start()
    ret_copy(3, 36, 12).wait_recv()
    merge(36, 15)
    lane = lax.broadcasted_iota(jnp.int32, (48, 128), 1)
    sub = lax.broadcasted_iota(jnp.int32, (48, 128), 0)
    for r in range(8):
        keep = jnp.sum(jnp.where(lane == sub, vflag[r : r + 1], 0.0), axis=1, keepdims=True)
        yext[43 + r, 0:48] = (yext[43 + r, 0:48].astype(F32) * keep).astype(BF)
    out_copy(3, 36, 15).start()

    for p in range(4):
        halo_copy(p).wait_send()
    ret_copy(0, 3, 9).wait_send()
    for p in range(1, 4):
        ret_copy(p, 12 * p, 12).wait_send()

    @pl.when(~south)
    def _():
        row_copy.wait_send()
        diag_copy.wait_send()

    @pl.when(~north)
    def _():
        below_copy.wait_send()
        corner_copy.wait_send()

    out_copy(0, 3, 9).wait()
    out_copy(1, 12, 12).wait()
    out_copy(2, 24, 12).wait()
    out_copy(3, 36, 15).wait()


def flag_rows(valid_ref, vhalo):
    parts = [valid_ref[40:48, :].astype(F32)]
    if vhalo is not None:
        parts += [vhalo[:, 0:HALO].astype(F32), jnp.zeros((8, 64), F32)]
    else:
        parts.append(jnp.zeros((8, 80), F32))
    return jnp.concatenate(parts, axis=1)


def deliver(src, dst, sem):
    copies = [
        pltpu.make_async_copy(src.at[pl.ds(6 * n, 6)], dst.at[pl.ds(6 * n, 6)], sem.at[n]) for n in range(8)
    ]
    for copy in copies:
        copy.start()
    for copy in copies:
        copy.wait()


def shards(tokens, valid, w_qkv, w_out, w_up, w_down):
    vmem = pl.BlockSpec(memory_space=pltpu.VMEM)
    hbm = pl.BlockSpec(memory_space=pl.ANY)
    dma = pltpu.SemaphoreType.DMA
    result = jax.ShapeDtypeStruct((48, 48, 512), BF)
    done = pl.pallas_call(
        kernel,
        out_shape=result,
        in_specs=[hbm, vmem] + [hbm] * 4 + [vmem],
        out_specs=hbm,
        scratch_shapes=[
            pltpu.VMEM((48, 48, 512), BF),
            pltpu.VMEM((51, EXT, 512), BF),
            pltpu.VMEM((51, EXT, 512), BF),
            pltpu.VMEM((51, HALO, 512), BF),
            pltpu.VMEM((8, 48), jnp.int32),
            pltpu.VMEM((2, 512, 1536), BF),
            pltpu.VMEM((2, 512, 512), BF),
            pltpu.VMEM((2, 512, 2048), BF),
            pltpu.VMEM((2, 2048, 512), BF),
            pltpu.VMEM((8, PAD, 1536), BF),
            pltpu.VMEM((576, 512), BF),
            pltpu.VMEM((576, 512), F32),
            pltpu.VMEM((576, 512), BF),
            pltpu.VMEM((576, 2048), BF),
            pltpu.VMEM((8, TOK, 256), F32),
            dma((4,)), dma((2, 4)), dma((4,)),
            dma((4,)), dma((4,)), dma(()), dma(()), dma(()), dma(()), dma(()), dma(()),
            dma((4,)), dma((4,)), dma(()), dma(()), dma(()), dma(()),
        ],
        compiler_params=pltpu.CompilerParams(
            collective_id=0, has_side_effects=True, vmem_limit_bytes=60 << 20
        ),
        name="swin",
    )(tokens, valid, w_qkv, w_out, w_up, w_down, jnp.asarray(head_sets(), BF))
    return pl.pallas_call(
        deliver,
        out_shape=result,
        in_specs=[hbm],
        out_specs=hbm,
        scratch_shapes=[dma((8,))],
        name="deliver",
    )(done)


def solution(mesh):
    return jax.shard_map(
        shards,
        mesh=mesh,
        in_specs=(P("lat", "lon", None), P("lat", "lon"), P(), P(), P(), P()),
        out_specs=P("lat", "lon", None),
        check_vma=False,
    )
```

```python
import jax
import jax.numpy as jnp
import numpy as np
from jax import lax
from jax.experimental import pallas as pl
from jax.experimental.pallas import tpu as pltpu
from jax.sharding import PartitionSpec as P

HEADS = 16
WIN_H = 6
WIN_W = 12
TOK = WIN_H * WIN_W
PAD = 80
EXT = 64
HALO = 16
MESH = pl.DeviceIdType.MESH
BF = jnp.bfloat16
F32 = jnp.float32


ORDER = [(0, 0), (0, 1), (0, 2), (1, 0), (1, 1), (1, 2), (0, 3), (1, 3)]
SCALE = 1.4426950408889634 * 32**-0.5


def head_sets():
    head = np.arange(256) // 32
    return np.stack([head // 3 == i for i in range(3)] + [head % 3 == j for j in range(3)])[:, None, :]


def layer_norm(wide):
    center = wide - jnp.mean(wide, axis=-1, keepdims=True)
    spread = jnp.mean(center * center, axis=-1, keepdims=True)
    return (center * lax.rsqrt(spread + 1e-05)).astype(BF)


def twice_gelu(x):
    return x + x * jnp.tanh(x * (0.7978845608028654 + 0.035677408136300125 * (x * x)))


def half_heads(q, k, v, sets, bias):
    by_key = jnp.concatenate([k * sets[i] for i in range(3)], 0)
    by_query = jnp.concatenate([q * sets[3 + j] for j in range(3)], 0)
    scores = lax.dot_general(by_key, by_query, (((1,), (1,)), ((), ())), preferred_element_type=F32)
    parts = []
    for i in range(3):
        part = scores[PAD * i : PAD * i + TOK]
        if bias is not None:
            part = part + bias
        largest = jnp.max(part, axis=0, keepdims=True)
        expo = jnp.exp2(part - largest)
        total = jnp.sum(expo, axis=0, keepdims=True)
        parts += [expo * (1.0 / total), jnp.zeros((PAD - TOK, 3 * PAD), F32)]
    probs = jnp.concatenate(parts, 0).astype(BF)
    by_value = jnp.concatenate([v * sets[i] for i in range(3)], 0)
    mixed = lax.dot_general(probs, by_value, (((0,), (0,)), ((), ())), preferred_element_type=F32)
    pick = [sets[3 + j].astype(F32) for j in range(3)]
    return (
        mixed[:TOK] * pick[0] + mixed[PAD : PAD + TOK] * pick[1] + mixed[2 * PAD : 2 * PAD + TOK] * pick[2]
    )


def window_bias(rows, first_col, halves=False):
    t = lax.broadcasted_iota(jnp.int32, (TOK, 128), 0)
    lane = lax.broadcasted_iota(jnp.int32, (TOK, 128), 1)
    tall = jnp.zeros((TOK, 128), F32)
    at = lane - first_col
    for half in range(2 if halves else 1):
        for r, row in enumerate(rows):
            low = (half * len(rows) + r) * WIN_W
            here = (t >= low) & (t < low + WIN_W) & (at == t - low + half * WIN_W)
            tall = jnp.where(here, row, tall)
    flag = jnp.sum(tall, axis=1, keepdims=True)
    key = lax.broadcasted_iota(jnp.int32, (TOK, 256), 0)
    query = lax.broadcasted_iota(jnp.int32, (TOK, 256), 1)
    query = query - PAD * ((query >= PAD).astype(jnp.int32) + (query >= 2 * PAD).astype(jnp.int32))
    allow = flag > 0.5
    if halves:
        allow = allow & ((key < TOK // 2) == (query < TOK // 2))
    allow = allow | (key == query) | (query >= TOK)
    return jnp.where(allow, 0.0, -jnp.inf)


def kernel(
    tok_hbm, valid_ref, wqkv_hbm, wout_hbm, wup_hbm, wdown_hbm, sets_ref,
    out_hbm,
    tok, ext, yext, ret, vhalo, wqkv, wout, wup, wdown, qkv, mixed, wide, resid, hidden, bias,
    tok_sem, w_sem, out_sem, halo_s, halo_r, row_s, row_r, diag_s, diag_r, v_s, v_r,
    ret_s, ret_r, corner_s, corner_r, below_s, below_r,
):
    lat, lon = lax.axis_index("lat"), lax.axis_index("lon")
    lats, lons = lax.axis_size("lat"), lax.axis_size("lon")
    north, south = lat == 0, lat == lats - 1
    left, right = lax.rem(lon + lons - 1, lons), lax.rem(lon + 1, lons)

    def tok_copy(p):
        return pltpu.make_async_copy(tok_hbm.at[pl.ds(12 * p, 12)], tok.at[pl.ds(12 * p, 12)], tok_sem.at[p])

    weights = [
        [
            pltpu.make_async_copy(src.at[b], dst.at[b], w_sem.at[b, n])
            for n, (src, dst) in enumerate(
                ((wqkv_hbm, wqkv), (wout_hbm, wout), (wup_hbm, wup), (wdown_hbm, wdown))
            )
        ]
        for b in range(2)
    ]
    tok_copy(3).start()
    for n in range(4):
        weights[0][n].start()
    for p in range(3):
        tok_copy(p).start()
    for n in range(4):
        weights[1][n].start()

    up, down = lax.rem(lat + lats - 1, lats), lax.rem(lat + 1, lats)
    barrier = pltpu.get_barrier_semaphore()
    for partner in ((lat, left), (lat, right), (up, lon), (up, right), (down, lon), (down, left)):
        place = {"lat": partner[0], "lon": partner[1]}
        pl.semaphore_signal(barrier, inc=1, device_id=place, device_id_type=MESH)

    qkv[:, TOK:PAD, :] = jnp.zeros((10, PAD - TOK, 1536), BF)
    bias[...] = jnp.zeros((10, TOK, 256), F32)

    @pl.when(north)
    def _():
        ext[0:3] = jnp.zeros((3, EXT, 512), BF)

    def send(src, dst, ssem, rsem, target):
        place = {"lat": target[0], "lon": target[1]}
        return pltpu.make_async_remote_copy(
            src_ref=src, dst_ref=dst, send_sem=ssem, recv_sem=rsem, device_id=place, device_id_type=MESH
        )

    v_copy = send(valid_ref.at[pl.ds(40, 8)], vhalo, v_s, v_r, (lat, left))

    def halo_copy(p):
        rows = pl.ds(3 + 12 * p, 12)
        return send(
            ext.at[rows, pl.ds(0, HALO)], ext.at[rows, pl.ds(48, HALO)], halo_s.at[p], halo_r.at[p], (lat, left)
        )

    row_copy = send(
        ext.at[pl.ds(48, 3), pl.ds(0, 48)], ext.at[pl.ds(0, 3), pl.ds(0, 48)], row_s, row_r, (lat + 1, lon)
    )
    diag_copy = send(
        ext.at[pl.ds(48, 3), pl.ds(0, HALO)], ext.at[pl.ds(0, 3), pl.ds(48, HALO)], diag_s, diag_r, (lat + 1, left)
    )

    def ret_copy(p, low, size):
        rows = pl.ds(low, size)
        return send(yext.at[rows, pl.ds(48, HALO)], ret.at[rows], ret_s.at[p], ret_r.at[p], (lat, right))

    below_copy = send(
        yext.at[pl.ds(0, 3), pl.ds(0, 48)], yext.at[pl.ds(48, 3), pl.ds(0, 48)], below_s, below_r, (lat - 1, lon)
    )
    corner_copy = send(
        yext.at[pl.ds(0, 3), pl.ds(48, HALO)], ret.at[pl.ds(48, 3)], corner_s, corner_r, (lat - 1, right)
    )
    pole_copy = send(
        yext.at[pl.ds(48, 3), pl.ds(48, HALO)], ret.at[pl.ds(48, 3)], corner_s, corner_r, (lat, right)
    )

    def out_copy(n, low, size):
        return pltpu.make_async_copy(
            yext.at[pl.ds(low, size), pl.ds(0, 48)], out_hbm.at[pl.ds(low - 3, size)], out_sem.at[n]
        )

    sets = [sets_ref[i] for i in range(6)]

    def gather0(p):
        x = tok[pl.ds(12 * p, 12)].astype(F32)
        for w, (band, j) in enumerate(ORDER):
            wide[TOK * w : TOK * w + TOK] = jnp.concatenate(
                [x[6 * band + r, 12 * j : 12 * j + 12] for r in range(6)], 0
            )

    def gather1(p):
        x = ext[pl.ds(12 * p, 12)].astype(F32)
        for w, (band, j) in enumerate(ORDER):
            wide[TOK * w : TOK * w + TOK] = jnp.concatenate(
                [x[6 * band + r, 12 * j + 6 : 12 * j + 18] for r in range(6)], 0
            )

    def project(b, x, tokens):
        out = jnp.dot(layer_norm(x), wqkv[b], preferred_element_type=F32)
        for w in range(tokens // TOK):
            rows = slice(TOK * w, TOK * w + TOK)
            qkv[w, 0:TOK, 0:512] = (out[rows, 0:512] * SCALE).astype(BF)
            qkv[w, 0:TOK, 512:1536] = out[rows, 512:1536].astype(BF)

    def attend(pair, masked):
        for g in range(2):
            both = []
            for w in (2 * pair, 2 * pair + 1):
                q = qkv[w, :, 256 * g : 256 * g + 256]
                k = qkv[w, :, 512 + 256 * g : 768 + 256 * g]
                v = qkv[w, :, 1024 + 256 * g : 1280 + 256 * g]
                both.append(half_heads(q, k, v, sets, bias[w, :, 0 : 3 * PAD] if masked else None))
            mixed[2 * TOK * pair : 2 * TOK * pair + 2 * TOK, 256 * g : 256 * g + 256] = jnp.concatenate(
                both, 0
            ).astype(BF)

    def add_mixed(b, rows):
        total = wide[rows] + jnp.dot(mixed[rows], wout[b], preferred_element_type=F32)
        total = total.astype(BF)
        resid[rows] = total
        return layer_norm(total.astype(F32))

    def expand(b, normed, rows, n):
        cut = slice(512 * n, 512 * n + 512)
        hidden[rows, cut] = twice_gelu(jnp.dot(normed, wup[b, :, cut], preferred_element_type=F32)).astype(BF)

    def contract(b, rows):
        return resid[rows].astype(F32) + 0.5 * jnp.dot(hidden[rows], wdown[b], preferred_element_type=F32)

    def scatter0(y, p):
        rows = [
            y[TOK * w + 12 * r : TOK * w + 12 * r + 12]
            for band in range(2)
            for r in range(6)
            for w in (ORDER.index((band, j)) for j in range(4))
        ]
        ext[pl.ds(3 + 12 * p, 12), 0:48] = jnp.concatenate(rows, 0).astype(BF).reshape(12, 48, 512)

    def scatter1(y, p):
        for band in range(2):
            for r in range(6):
                row = [y[TOK * w + 12 * r : TOK * w + 12 * r + 12] for w in (ORDER.index((band, j)) for j in range(4))]
                row = [jnp.zeros((6, 512), F32)] + row + [jnp.zeros((10, 512), F32)]
                yext[12 * p + 6 * band + r] = jnp.concatenate(row, 0).astype(BF)

    everything = slice(0, 576)

    def step(b_feed, p_feed, b_att, gather, p_att, scatter, masked=False, edge=False):
        normed = add_mixed(b_feed, everything)
        gather(p_att)
        project(b_att, wide[0:720] if edge else wide[0:576], 720 if edge else 576)
        for n in range(4):
            expand(b_feed, normed, everything, n)
            attend(n, masked)
        if edge:
            attend(4, masked)
        scatter(contract(b_feed, everything), p_feed)

    vflag = flag_rows(valid_ref, None)

    @pl.when(south)
    def _():
        for w, (band, j) in enumerate(ORDER):
            if band == 1:
                bias[w] = window_bias([vflag[r : r + 1] for r in range(2, 8)], 12 * j)

    tok_copy(3).wait()
    weights[0][0].wait()
    gather0(3)
    project(0, wide[0:576], 576)
    for n in range(4):
        attend(n, True)

    @pl.when(south)
    def _():
        for w, (band, j) in enumerate(ORDER):
            if band == 1:
                bias[w] = jnp.zeros((TOK, 256), F32)

    for n in range(1, 4):
        weights[0][n].wait()
    pl.semaphore_wait(barrier, 6)
    v_copy.start()

    def block0(p, carry):
        tok_copy(p).wait()
        before = lax.rem(p + 3, 4)
        step(0, before, 0, gather0, p, scatter0)

        @pl.when((p == 0) & ~south)
        def _():
            row_copy.start()
            diag_copy.start()

        halo_copy(before).start()
        return carry

    lax.fori_loop(0, 3, block0, 0)

    v_copy.wait()
    vflag = flag_rows(valid_ref, vhalo)
    one = jnp.ones((1, 128), F32)
    for n in range(4):
        weights[1][n].wait()

    @pl.when(north)
    def _():
        for w, (band, j) in enumerate(ORDER):
            if band == 0:
                bias[w] = window_bias([0.0 * one] * 3 + [one] * 3, 6 + 12 * j)

    @pl.when(~north)
    def _():
        row_copy.wait_recv()
        diag_copy.wait_recv()

    halo_copy(3).wait_recv()
    halo_copy(0).wait_recv()
    step(0, 2, 1, gather1, 0, scatter0, masked=True)
    halo_copy(2).start()

    @pl.when(north)
    def _():
        for w, (band, j) in enumerate(ORDER):
            if band == 0:
                bias[w] = jnp.zeros((TOK, 256), F32)

    def merge(low, size):
        rows = pl.ds(low, size)
        col = lax.broadcasted_iota(jnp.int32, (1, HALO, 512), 1)
        yext[rows, 0:HALO] = jnp.where(
            col < 6, ret[rows].astype(F32), yext[rows, 0:HALO].astype(F32)
        ).astype(BF)

    def block1(p, carry):
        halo_copy(p).wait_recv()
        step(1, p - 1, 1, gather1, p, scatter1)

        @pl.when(p == 1)
        def _():
            ret_copy(0, 3, 9).start()

            @pl.when(~north)
            def _():
                below_copy.start()
                corner_copy.start()

        @pl.when(p == 2)
        def _():
            ret_copy(1, 12, 12).start()
            ret_copy(0, 3, 9).wait_recv()
            merge(3, 9)
            out_copy(0, 3, 9).start()

        return carry

    lax.fori_loop(1, 3, block1, 0)

    @pl.when(south)
    def _():
        for w, (band, j) in enumerate(ORDER):
            if band == 1:
                bias[w] = window_bias([one] + [vflag[r : r + 1] for r in range(5)], 6 + 12 * j)

    for w in range(2):
        bias[8 + w] = window_bias([vflag[r : r + 1] for r in range(5, 8)], 6 + 24 * w, halves=True)

    def gather_last(p):
        gather1(p)
        x = ext[48:51].astype(F32)
        wide[8 * TOK : 10 * TOK] = jnp.concatenate(
            [x[r, 12 * j + 6 : 12 * j + 18] for j in range(4) for r in range(3)], 0
        )

    step(1, 2, 1, gather_last, 3, scatter1, masked=True, edge=True)
    ret_copy(2, 24, 12).start()
    ret_copy(1, 12, 12).wait_recv()
    merge(12, 12)
    out_copy(1, 12, 12).start()

    others, first = slice(0, 6 * TOK), slice(6 * TOK, 10 * TOK)
    normed = add_mixed(1, first)
    for n in range(4):
        expand(1, normed, first, n)
    y = contract(1, first)
    for band in range(2):
        for r in range(6):
            row = [y[TOK * band + 12 * r + 6 : TOK * band + 12 * r + 12], jnp.zeros((10, 512), F32)]
            yext[36 + 6 * band + r, 48:64] = jnp.concatenate(row, 0).astype(BF)

    @pl.when(south)
    def _():
        for r in range(3):
            row = [y[2 * TOK + 36 * j + 12 * r : 2 * TOK + 36 * j + 12 * r + 12] for j in range(4)]
            row = [jnp.zeros((6, 512), F32)] + row + [jnp.zeros((10, 512), F32)]
            yext[48 + r] = jnp.concatenate(row, 0).astype(BF)
        pole_copy.start()

    ret_copy(3, 36, 12).start()
    normed = add_mixed(1, others)
    for n in range(4):
        expand(1, normed, others, n)
    y = jnp.concatenate([contract(1, others), y[0 : 2 * TOK]], 0)
    for band in range(2):
        for r in range(6):
            row = [y[TOK * w + 12 * r : TOK * w + 12 * r + 12] for w in (ORDER.index((band, j)) for j in range(4))]
            row = [jnp.zeros((6, 512), F32)] + row
            yext[36 + 6 * band + r, 0:48] = jnp.concatenate(row, 0)[0:48].astype(BF)

    @pl.when(south)
    def _():
        pole_copy.wait()

    @pl.when(~south)
    def _():
        below_copy.wait_recv()
        corner_copy.wait_recv()

    ret_copy(2, 24, 12).wait_recv()
    merge(24, 12)
    out_copy(2, 24, 12).start()
    ret_copy(3, 36, 12).wait_recv()
    merge(36, 15)
    lane = lax.broadcasted_iota(jnp.int32, (48, 128), 1)
    sub = lax.broadcasted_iota(jnp.int32, (48, 128), 0)
    for r in range(8):
        keep = jnp.sum(jnp.where(lane == sub, vflag[r : r + 1], 0.0), axis=1, keepdims=True)
        yext[43 + r, 0:48] = (yext[43 + r, 0:48].astype(F32) * keep).astype(BF)
    out_copy(3, 36, 15).start()

    for p in range(4):
        halo_copy(p).wait_send()
    ret_copy(0, 3, 9).wait_send()
    for p in range(1, 4):
        ret_copy(p, 12 * p, 12).wait_send()

    @pl.when(~south)
    def _():
        row_copy.wait_send()
        diag_copy.wait_send()

    @pl.when(~north)
    def _():
        below_copy.wait_send()
        corner_copy.wait_send()

    out_copy(0, 3, 9).wait()
    out_copy(1, 12, 12).wait()
    out_copy(2, 24, 12).wait()
    out_copy(3, 36, 15).wait()


def flag_rows(valid_ref, vhalo):
    parts = [valid_ref[40:48, :].astype(F32)]
    if vhalo is not None:
        parts += [vhalo[:, 0:HALO].astype(F32), jnp.zeros((8, 64), F32)]
    else:
        parts.append(jnp.zeros((8, 80), F32))
    return jnp.concatenate(parts, axis=1)


def deliver(src, dst, held, load_sem, store_sem):
    parts = [pl.ds(6 * n, 6) for n in range(8)]
    loads = [pltpu.make_async_copy(src.at[part], held.at[part], load_sem.at[n]) for n, part in enumerate(parts)]
    stores = [pltpu.make_async_copy(held.at[part], dst.at[part], store_sem.at[n]) for n, part in enumerate(parts)]
    for load in loads:
        load.start()
    for load, store in zip(loads, stores):
        load.wait()
        store.start()
    for store in stores:
        store.wait()


def shards(tokens, valid, w_qkv, w_out, w_up, w_down):
    vmem = pl.BlockSpec(memory_space=pltpu.VMEM)
    hbm = pl.BlockSpec(memory_space=pl.ANY)
    dma = pltpu.SemaphoreType.DMA
    result = jax.ShapeDtypeStruct((48, 48, 512), BF)
    done = pl.pallas_call(
        kernel,
        out_shape=result,
        in_specs=[hbm, vmem] + [hbm] * 4 + [vmem],
        out_specs=hbm,
        scratch_shapes=[
            pltpu.VMEM((48, 48, 512), BF),
            pltpu.VMEM((51, EXT, 512), BF),
            pltpu.VMEM((51, EXT, 512), BF),
            pltpu.VMEM((51, HALO, 512), BF),
            pltpu.VMEM((8, 48), jnp.int32),
            pltpu.VMEM((2, 512, 1536), BF),
            pltpu.VMEM((2, 512, 512), BF),
            pltpu.VMEM((2, 512, 2048), BF),
            pltpu.VMEM((2, 2048, 512), BF),
            pltpu.VMEM((10, PAD, 1536), BF),
            pltpu.VMEM((720, 512), BF),
            pltpu.VMEM((720, 512), F32),
            pltpu.VMEM((720, 512), BF),
            pltpu.VMEM((720, 2048), BF),
            pltpu.VMEM((10, TOK, 256), F32),
            dma((4,)), dma((2, 4)), dma((4,)),
            dma((4,)), dma((4,)), dma(()), dma(()), dma(()), dma(()), dma(()), dma(()),
            dma((4,)), dma((4,)), dma(()), dma(()), dma(()), dma(()),
        ],
        compiler_params=pltpu.CompilerParams(
            collective_id=0, has_side_effects=True, vmem_limit_bytes=60 << 20
        ),
        name="swin",
    )(tokens, valid, w_qkv, w_out, w_up, w_down, jnp.asarray(head_sets(), BF))
    return pl.pallas_call(
        deliver,
        out_shape=result,
        in_specs=[hbm],
        out_specs=hbm,
        scratch_shapes=[pltpu.VMEM((48, 48, 512), BF), dma((8,)), dma((8,))],
        name="deliver",
    )(done)


def solution(mesh):
    return jax.shard_map(
        shards,
        mesh=mesh,
        in_specs=(P("lat", "lon", None), P("lat", "lon"), P(), P(), P(), P()),
        out_specs=P("lat", "lon", None),
        check_vma=False,
    )
```

```python
import jax
import jax.numpy as jnp
import numpy as np
from jax import lax
from jax.experimental import pallas as pl
from jax.experimental.pallas import tpu as pltpu
from jax.sharding import PartitionSpec as P

HEADS = 16
WIN_H = 6
WIN_W = 12
TOK = WIN_H * WIN_W
PAD = 80
EXT = 64
HALO = 16
MESH = pl.DeviceIdType.MESH
BF = jnp.bfloat16
F32 = jnp.float32


ORDER = [(0, 0), (0, 1), (0, 2), (1, 0), (1, 1), (1, 2), (0, 3), (1, 3)]
SCALE = 1.4426950408889634 * 32**-0.5


def head_sets():
    head = np.arange(256) // 32
    return np.stack([head // 3 == i for i in range(3)] + [head % 3 == j for j in range(3)])[:, None, :]


def layer_norm(wide):
    center = wide - jnp.mean(wide, axis=-1, keepdims=True)
    spread = jnp.mean(center * center, axis=-1, keepdims=True)
    return (center * lax.rsqrt(spread + 1e-05)).astype(BF)


def twice_gelu(x):
    return x + x * jnp.tanh(x * (0.7978845608028654 + 0.035677408136300125 * (x * x)))


def half_heads(q, k, v, sets, bias):
    by_key = jnp.concatenate([k * sets[i] for i in range(3)], 0)
    by_query = jnp.concatenate([q * sets[3 + j] for j in range(3)], 0)
    scores = lax.dot_general(by_key, by_query, (((1,), (1,)), ((), ())), preferred_element_type=F32)
    parts = []
    for i in range(3):
        part = scores[PAD * i : PAD * i + TOK]
        if bias is not None:
            part = part + bias
        largest = jnp.max(part, axis=0, keepdims=True)
        expo = jnp.exp2((part - largest) * SCALE)
        total = jnp.sum(expo, axis=0, keepdims=True)
        parts += [expo * (1.0 / total), jnp.zeros((PAD - TOK, 3 * PAD), F32)]
    probs = jnp.concatenate(parts, 0).astype(BF)
    by_value = jnp.concatenate([v * sets[i] for i in range(3)], 0)
    mixed = lax.dot_general(probs, by_value, (((0,), (0,)), ((), ())), preferred_element_type=F32)
    pick = [sets[3 + j].astype(F32) for j in range(3)]
    return (
        mixed[:TOK] * pick[0] + mixed[PAD : PAD + TOK] * pick[1] + mixed[2 * PAD : 2 * PAD + TOK] * pick[2]
    )


def window_bias(rows, first_col, halves=False):
    t = lax.broadcasted_iota(jnp.int32, (TOK, 128), 0)
    lane = lax.broadcasted_iota(jnp.int32, (TOK, 128), 1)
    tall = jnp.zeros((TOK, 128), F32)
    at = lane - first_col
    for half in range(2 if halves else 1):
        for r, row in enumerate(rows):
            low = (half * len(rows) + r) * WIN_W
            here = (t >= low) & (t < low + WIN_W) & (at == t - low + half * WIN_W)
            tall = jnp.where(here, row, tall)
    flag = jnp.sum(tall, axis=1, keepdims=True)
    key = lax.broadcasted_iota(jnp.int32, (TOK, 256), 0)
    query = lax.broadcasted_iota(jnp.int32, (TOK, 256), 1)
    query = query - PAD * ((query >= PAD).astype(jnp.int32) + (query >= 2 * PAD).astype(jnp.int32))
    allow = flag > 0.5
    if halves:
        allow = allow & ((key < TOK // 2) == (query < TOK // 2))
    allow = allow | (key == query) | (query >= TOK)
    return jnp.where(allow, 0.0, -jnp.inf)


def kernel(
    tok_hbm, valid_ref, wqkv_hbm, wout_hbm, wup_hbm, wdown_hbm, sets_ref,
    out_hbm,
    tok, ext, yext, outgoing, ret, edge_out, edge_in, vhalo, wqkv, wout, wup, wdown, qkv, mixed, wide, resid, hidden, bias,
    tok_sem, w_sem, out_sem, halo_s, halo_r, row_s, row_r, diag_s, diag_r, v_s, v_r,
    ret_s, ret_r, corner_s, corner_r, pole_s, below_s, below_r,
):
    lat, lon = lax.axis_index("lat"), lax.axis_index("lon")
    lats, lons = lax.axis_size("lat"), lax.axis_size("lon")
    north, south = lat == 0, lat == lats - 1
    left, right = lax.rem(lon + lons - 1, lons), lax.rem(lon + 1, lons)

    def tok_copy(p):
        return pltpu.make_async_copy(tok_hbm.at[pl.ds(12 * p, 12)], tok.at[pl.ds(12 * p, 12)], tok_sem.at[p])

    weights = [
        [
            pltpu.make_async_copy(src.at[b], dst.at[b], w_sem.at[b, n])
            for n, (src, dst) in enumerate(
                ((wqkv_hbm, wqkv), (wout_hbm, wout), (wup_hbm, wup), (wdown_hbm, wdown))
            )
        ]
        for b in range(2)
    ]
    tok_copy(3).start()
    for n in range(4):
        weights[0][n].start()
    for p in range(3):
        tok_copy(p).start()
    for n in range(4):
        weights[1][n].start()

    up, down = lax.rem(lat + lats - 1, lats), lax.rem(lat + 1, lats)
    barrier = pltpu.get_barrier_semaphore()
    for partner in ((lat, left), (lat, right), (up, lon), (up, right), (down, lon), (down, left)):
        place = {"lat": partner[0], "lon": partner[1]}
        pl.semaphore_signal(barrier, inc=1, device_id=place, device_id_type=MESH)

    qkv[:, TOK:PAD, :] = jnp.zeros((10, PAD - TOK, 1536), BF)
    bias[...] = jnp.zeros((26, TOK, 256), F32)
    one = jnp.ones((1, 128), F32)
    vflag = flag_rows(valid_ref, None)

    @pl.when(south)
    def _():
        for w, (band, j) in enumerate(ORDER):
            if band == 1:
                bias[w] = window_bias([vflag[r : r + 1] for r in range(2, 8)], 12 * j)

    @pl.when(north)
    def _():
        for w, (band, j) in enumerate(ORDER):
            if band == 0:
                bias[8 + w] = window_bias([0.0 * one] * 3 + [one] * 3, 6 + 12 * j)

    @pl.when(north)
    def _():
        ext[0:3] = jnp.zeros((3, EXT, 512), BF)

    def send(src, dst, ssem, rsem, target):
        place = {"lat": target[0], "lon": target[1]}
        return pltpu.make_async_remote_copy(
            src_ref=src, dst_ref=dst, send_sem=ssem, recv_sem=rsem, device_id=place, device_id_type=MESH
        )

    v_copy = send(valid_ref.at[pl.ds(40, 8)], vhalo, v_s, v_r, (lat, left))

    def halo_copy(p):
        rows = pl.ds(3 + 12 * p, 12)
        return send(
            ext.at[rows, pl.ds(0, HALO)], ext.at[rows, pl.ds(48, HALO)], halo_s.at[p], halo_r.at[p], (lat, left)
        )

    row_copy = send(
        ext.at[pl.ds(48, 3), pl.ds(0, 48)], ext.at[pl.ds(0, 3), pl.ds(0, 48)], row_s, row_r, (lat + 1, lon)
    )
    diag_copy = send(
        ext.at[pl.ds(48, 3), pl.ds(0, HALO)], ext.at[pl.ds(0, 3), pl.ds(48, HALO)], diag_s, diag_r, (lat + 1, left)
    )

    def ret_copy(p):
        return send(outgoing.at[p], ret.at[p], ret_s.at[p], ret_r.at[p], (lat, right))

    below_copy = send(yext.at[pl.ds(0, 3)], yext.at[pl.ds(48, 3)], below_s, below_r, (lat - 1, lon))
    corner_copy = send(outgoing.at[0, pl.ds(0, 32)], edge_in, corner_s, corner_r, (lat - 1, right))
    pole_copy = send(edge_out, edge_in, pole_s, corner_r, (lat, right))

    def out_copy(n, low, size):
        return pltpu.make_async_copy(
            yext.at[pl.ds(low, size)], out_hbm.at[pl.ds(low - 3, size)], out_sem.at[n]
        )

    sets = [sets_ref[i] for i in range(6)]

    def gather0(p):
        x = tok[pl.ds(12 * p, 12)].astype(F32)
        for w, (band, j) in enumerate(ORDER):
            wide[TOK * w : TOK * w + TOK] = jnp.concatenate(
                [x[6 * band + r, 12 * j : 12 * j + 12] for r in range(6)], 0
            )

    def gather1(p):
        x = ext[pl.ds(12 * p, 12)].astype(F32)
        for w, (band, j) in enumerate(ORDER):
            wide[TOK * w : TOK * w + TOK] = jnp.concatenate(
                [x[6 * band + r, 12 * j + 6 : 12 * j + 18] for r in range(6)], 0
            )

    def project(b, x, tokens):
        out = jnp.dot(layer_norm(x), wqkv[b], preferred_element_type=F32)
        for w in range(tokens // TOK):
            qkv[w, 0:TOK, :] = out[TOK * w : TOK * w + TOK].astype(BF)

    def attend(pair, flagged):
        for g in range(2):
            both = []
            for w in (2 * pair, 2 * pair + 1):
                q = qkv[w, :, 256 * g : 256 * g + 256]
                k = qkv[w, :, 512 + 256 * g : 768 + 256 * g]
                v = qkv[w, :, 1024 + 256 * g : 1280 + 256 * g]
                both.append(half_heads(q, k, v, sets, None if flagged is None else bias[flagged + w, :, 0 : 3 * PAD]))
            mixed[2 * TOK * pair : 2 * TOK * pair + 2 * TOK, 256 * g : 256 * g + 256] = jnp.concatenate(
                both, 0
            ).astype(BF)

    def add_mixed(b, rows):
        total = wide[rows] + jnp.dot(mixed[rows], wout[b], preferred_element_type=F32)
        total = total.astype(BF)
        resid[rows] = total
        return layer_norm(total.astype(F32))

    def expand(b, normed, rows, n):
        cut = slice(512 * n, 512 * n + 512)
        hidden[rows, cut] = twice_gelu(jnp.dot(normed, wup[b, :, cut], preferred_element_type=F32)).astype(BF)

    def contract(b, rows):
        return resid[rows].astype(F32) + 0.5 * jnp.dot(hidden[rows], wdown[b], preferred_element_type=F32)

    def scatter0(y, p):
        rows = [
            y[TOK * w + 12 * r : TOK * w + 12 * r + 12]
            for band in range(2)
            for r in range(6)
            for w in (ORDER.index((band, j)) for j in range(4))
        ]
        ext[pl.ds(3 + 12 * p, 12), 0:48] = jnp.concatenate(rows, 0).astype(BF).reshape(12, 48, 512)

    def pack(y, p):
        part = [y[TOK * band + 12 * r + 6 : TOK * band + 12 * r + 12] for band in range(2) for r in range(6)]
        outgoing[p] = jnp.concatenate(part + [jnp.zeros((PAD - TOK, 512), F32)], 0).astype(BF)

    def settle(y, p):
        for band in range(2):
            for r in range(6):
                row = [y[TOK * w + 12 * r : TOK * w + 12 * r + 12] for w in (ORDER.index((band, j)) for j in range(4))]
                row = [jnp.zeros((6, 512), F32)] + row
                yext[12 * p + 6 * band + r] = jnp.concatenate(row, 0)[0:48].astype(BF)

    def scatter1(y, p):
        pack(y[6 * TOK : 8 * TOK], p)
        settle(y, p)

    everything = slice(0, 576)

    def step(b_feed, p_feed, b_att, gather, p_att, scatter, flagged=None, edge=False):
        normed = add_mixed(b_feed, everything)
        gather(p_att)
        project(b_att, wide[0:720] if edge else wide[0:576], 720 if edge else 576)
        for n in range(4):
            expand(b_feed, normed, everything, n)
            attend(n, flagged)
        if edge:
            attend(4, flagged)
        scatter(contract(b_feed, everything), p_feed)

    tok_copy(3).wait()
    weights[0][0].wait()
    gather0(3)
    project(0, wide[0:576], 576)
    for n in range(4):
        attend(n, 0)

    for n in range(1, 4):
        weights[0][n].wait()
    pl.semaphore_wait(barrier, 6)
    v_copy.start()

    def block0(p, carry):
        tok_copy(p).wait()
        before = lax.rem(p + 3, 4)
        step(0, before, 0, gather0, p, scatter0)

        @pl.when((p == 0) & ~south)
        def _():
            row_copy.start()
            diag_copy.start()

        halo_copy(before).start()
        return carry

    lax.fori_loop(0, 3, block0, 0)

    v_copy.wait()
    vflag = flag_rows(valid_ref, vhalo)
    for n in range(4):
        weights[1][n].wait()

    @pl.when(south)
    def _():
        for w, (band, j) in enumerate(ORDER):
            if band == 1:
                bias[16 + w] = window_bias([one] + [vflag[r : r + 1] for r in range(5)], 6 + 12 * j)
        for w in range(2):
            bias[24 + w] = window_bias([vflag[r : r + 1] for r in range(5, 8)], 6 + 24 * w, halves=True)

    @pl.when(~north)
    def _():
        row_copy.wait_recv()
        diag_copy.wait_recv()

    halo_copy(3).wait_recv()
    halo_copy(0).wait_recv()
    step(0, 2, 1, gather1, 0, scatter0, flagged=8)
    halo_copy(2).start()

    def merge(low, count, source):
        came = source.astype(F32)
        for r in range(count):
            own = yext[low + r, 0:HALO].astype(F32)
            yext[low + r, 0:HALO] = jnp.concatenate([came[6 * r : 6 * r + 6], own[6:]], 0).astype(BF)

    def block1(p, carry):
        halo_copy(p).wait_recv()
        step(1, p - 1, 1, gather1, p, scatter1)

        @pl.when(p == 1)
        def _():
            ret_copy(0).start()

            @pl.when(~north)
            def _():
                below_copy.start()
                corner_copy.start()

        @pl.when(p == 2)
        def _():
            ret_copy(1).start()
            ret_copy(0).wait_recv()
            merge(3, 9, ret[0, 18:72])
            out_copy(0, 3, 9).start()

        return carry

    lax.fori_loop(1, 3, block1, 0)

    def gather_last(p):
        gather1(p)
        x = ext[48:51].astype(F32)
        wide[8 * TOK : 10 * TOK] = jnp.concatenate(
            [x[r, 12 * j + 6 : 12 * j + 18] for j in range(4) for r in range(3)], 0
        )

    step(1, 2, 1, gather_last, 3, scatter1, flagged=16, edge=True)
    ret_copy(2).start()
    ret_copy(1).wait_recv()
    merge(12, 12, ret[1])
    out_copy(1, 12, 12).start()

    others, first = slice(0, 6 * TOK), slice(6 * TOK, 10 * TOK)
    normed = add_mixed(1, first)
    for n in range(4):
        expand(1, normed, first, n)
    y = contract(1, first)
    pack(y[0 : 2 * TOK], 3)

    @pl.when(south)
    def _():
        part = [y[2 * TOK + 108 + 12 * r + 6 : 2 * TOK + 108 + 12 * r + 12] for r in range(3)]
        edge_out[...] = jnp.concatenate(part + [jnp.zeros((14, 512), F32)], 0).astype(BF)
        pole_copy.start()
        for r in range(3):
            row = [y[2 * TOK + 36 * j + 12 * r : 2 * TOK + 36 * j + 12 * r + 12] for j in range(4)]
            yext[48 + r] = jnp.concatenate([jnp.zeros((6, 512), F32)] + row, 0)[0:48].astype(BF)

    ret_copy(3).start()
    normed = add_mixed(1, others)
    for n in range(4):
        expand(1, normed, others, n)
    settle(jnp.concatenate([contract(1, others), y[0 : 2 * TOK]], 0), 3)

    @pl.when(south)
    def _():
        pole_copy.wait()

    @pl.when(~south)
    def _():
        below_copy.wait_recv()
        corner_copy.wait_recv()

    ret_copy(2).wait_recv()
    merge(24, 12, ret[2])
    out_copy(2, 24, 12).start()
    ret_copy(3).wait_recv()
    merge(36, 12, ret[3])
    merge(48, 3, edge_in[...])
    lane = lax.broadcasted_iota(jnp.int32, (48, 128), 1)
    sub = lax.broadcasted_iota(jnp.int32, (48, 128), 0)
    for r in range(8):
        keep = jnp.sum(jnp.where(lane == sub, vflag[r : r + 1], 0.0), axis=1, keepdims=True)
        yext[43 + r] = (yext[43 + r].astype(F32) * keep).astype(BF)
    out_copy(3, 36, 15).start()

    for p in range(4):
        halo_copy(p).wait_send()
        ret_copy(p).wait_send()

    @pl.when(~south)
    def _():
        row_copy.wait_send()
        diag_copy.wait_send()

    @pl.when(~north)
    def _():
        below_copy.wait_send()
        corner_copy.wait_send()

    out_copy(0, 3, 9).wait()
    out_copy(1, 12, 12).wait()
    out_copy(2, 24, 12).wait()
    out_copy(3, 36, 15).wait()


def flag_rows(valid_ref, vhalo):
    parts = [valid_ref[40:48, :].astype(F32)]
    if vhalo is not None:
        parts += [vhalo[:, 0:HALO].astype(F32), jnp.zeros((8, 64), F32)]
    else:
        parts.append(jnp.zeros((8, 80), F32))
    return jnp.concatenate(parts, axis=1)


def deliver(src, dst, held, load_sem, store_sem):
    parts = [pl.ds(6 * n, 6) for n in range(8)]
    loads = [pltpu.make_async_copy(src.at[part], held.at[part], load_sem.at[n]) for n, part in enumerate(parts)]
    stores = [pltpu.make_async_copy(held.at[part], dst.at[part], store_sem.at[n]) for n, part in enumerate(parts)]
    for load in loads:
        load.start()
    for load, store in zip(loads, stores):
        load.wait()
        store.start()
    for store in stores:
        store.wait()


def shards(tokens, valid, w_qkv, w_out, w_up, w_down):
    vmem = pl.BlockSpec(memory_space=pltpu.VMEM)
    hbm = pl.BlockSpec(memory_space=pl.ANY)
    dma = pltpu.SemaphoreType.DMA
    result = jax.ShapeDtypeStruct((48, 48, 512), BF)
    done = pl.pallas_call(
        kernel,
        out_shape=result,
        in_specs=[hbm, vmem] + [hbm] * 4 + [vmem],
        out_specs=hbm,
        scratch_shapes=[
            pltpu.VMEM((48, 48, 512), BF),
            pltpu.VMEM((51, EXT, 512), BF),
            pltpu.VMEM((51, 48, 512), BF),
            pltpu.VMEM((4, PAD, 512), BF),
            pltpu.VMEM((4, PAD, 512), BF),
            pltpu.VMEM((32, 512), BF),
            pltpu.VMEM((32, 512), BF),
            pltpu.VMEM((8, 48), jnp.int32),
            pltpu.VMEM((2, 512, 1536), BF),
            pltpu.VMEM((2, 512, 512), BF),
            pltpu.VMEM((2, 512, 2048), BF),
            pltpu.VMEM((2, 2048, 512), BF),
            pltpu.VMEM((10, PAD, 1536), BF),
            pltpu.VMEM((720, 512), BF),
            pltpu.VMEM((720, 512), F32),
            pltpu.VMEM((720, 512), BF),
            pltpu.VMEM((720, 2048), BF),
            pltpu.VMEM((26, TOK, 256), F32),
            dma((4,)), dma((2, 4)), dma((4,)),
            dma((4,)), dma((4,)), dma(()), dma(()), dma(()), dma(()), dma(()), dma(()),
            dma((4,)), dma((4,)), dma(()), dma(()), dma(()), dma(()), dma(()),
        ],
        compiler_params=pltpu.CompilerParams(
            collective_id=0, has_side_effects=True, vmem_limit_bytes=60 << 20
        ),
        name="swin",
    )(tokens, valid, w_qkv, w_out, w_up, w_down, jnp.asarray(head_sets(), BF))
    return pl.pallas_call(
        deliver,
        out_shape=result,
        in_specs=[hbm],
        out_specs=hbm,
        scratch_shapes=[pltpu.VMEM((48, 48, 512), BF), dma((8,)), dma((8,))],
        name="deliver",
    )(done)


def solution(mesh):
    return jax.shard_map(
        shards,
        mesh=mesh,
        in_specs=(P("lat", "lon", None), P("lat", "lon"), P(), P(), P(), P()),
        out_specs=P("lat", "lon", None),
        check_vma=False,
    )
```

```python
import jax
import jax.numpy as jnp
import numpy as np
from jax import lax
from jax.experimental import pallas as pl
from jax.experimental.pallas import tpu as pltpu
from jax.sharding import PartitionSpec as P

HEADS = 16
WIN_H = 6
WIN_W = 12
TOK = WIN_H * WIN_W
PAD = 80
HALO = 16
MESH = pl.DeviceIdType.MESH
BF = jnp.bfloat16
F32 = jnp.float32


ORDER = [(0, 0), (0, 1), (0, 2), (1, 0), (1, 1), (1, 2), (0, 3), (1, 3)]
INNER = ORDER[:6]
SCALE = 1.4426950408889634 * 32**-0.5


def head_sets():
    head = np.arange(256) // 32
    return np.stack([head // 3 == i for i in range(3)] + [head % 3 == j for j in range(3)])[:, None, :]


def layer_norm(wide):
    center = wide - jnp.mean(wide, axis=-1, keepdims=True)
    spread = jnp.mean(center * center, axis=-1, keepdims=True)
    return (center * lax.rsqrt(spread + 1e-05)).astype(BF)


def twice_gelu(x):
    return x + x * jnp.tanh(x * (0.7978845608028654 + 0.035677408136300125 * (x * x)))


def half_heads(q, k, v, sets, bias):
    by_key = jnp.concatenate([k * sets[i] for i in range(3)], 0)
    by_query = jnp.concatenate([q * sets[3 + j] for j in range(3)], 0)
    scores = lax.dot_general(by_key, by_query, (((1,), (1,)), ((), ())), preferred_element_type=F32)
    parts = []
    for i in range(3):
        part = scores[PAD * i : PAD * i + TOK]
        if bias is not None:
            part = part + bias
        largest = jnp.max(part, axis=0, keepdims=True)
        expo = jnp.exp2((part - largest) * SCALE)
        total = jnp.sum(expo, axis=0, keepdims=True)
        parts += [expo * (1.0 / total), jnp.zeros((PAD - TOK, 3 * PAD), F32)]
    probs = jnp.concatenate(parts, 0).astype(BF)
    by_value = jnp.concatenate([v * sets[i] for i in range(3)], 0)
    mixed = lax.dot_general(probs, by_value, (((0,), (0,)), ((), ())), preferred_element_type=F32)
    pick = [sets[3 + j].astype(F32) for j in range(3)]
    return (
        mixed[:TOK] * pick[0] + mixed[PAD : PAD + TOK] * pick[1] + mixed[2 * PAD : 2 * PAD + TOK] * pick[2]
    )


def window_bias(rows, first_col, halves=False):
    t = lax.broadcasted_iota(jnp.int32, (TOK, 128), 0)
    lane = lax.broadcasted_iota(jnp.int32, (TOK, 128), 1)
    tall = jnp.zeros((TOK, 128), F32)
    at = lane - first_col
    for half in range(2 if halves else 1):
        for r, row in enumerate(rows):
            low = (half * len(rows) + r) * WIN_W
            here = (t >= low) & (t < low + WIN_W) & (at == t - low + half * WIN_W)
            tall = jnp.where(here, row, tall)
    flag = jnp.sum(tall, axis=1, keepdims=True)
    key = lax.broadcasted_iota(jnp.int32, (TOK, 256), 0)
    query = lax.broadcasted_iota(jnp.int32, (TOK, 256), 1)
    query = query - PAD * ((query >= PAD).astype(jnp.int32) + (query >= 2 * PAD).astype(jnp.int32))
    allow = flag > 0.5
    if halves:
        allow = allow & ((key < TOK // 2) == (query < TOK // 2))
    allow = allow | (key == query) | (query >= TOK)
    return jnp.where(allow, 0.0, -jnp.inf)


def kernel(
    tok_hbm, valid_ref, wqkv_hbm, wout_hbm, wup_hbm, wdown_hbm, sets_ref,
    out_hbm,
    tok, ext, yext, halo_out, halo_in, diag_in, inner, outgoing, ret, edge_out, edge_in, vhalo, wqkv, wout, wup, wdown, qkv, mixed, wide, resid, hidden, bias,
    tok_sem, w_sem, out_sem, halo_s, halo_r, row_s, row_r, diag_s, diag_r, v_s, v_r,
    ret_s, ret_r, corner_s, corner_r, pole_s, below_s, below_r,
):
    lat, lon = lax.axis_index("lat"), lax.axis_index("lon")
    lats, lons = lax.axis_size("lat"), lax.axis_size("lon")
    north, south = lat == 0, lat == lats - 1
    left, right = lax.rem(lon + lons - 1, lons), lax.rem(lon + 1, lons)

    def tok_copy(p):
        return pltpu.make_async_copy(tok_hbm.at[pl.ds(12 * p, 12)], tok.at[pl.ds(12 * p, 12)], tok_sem.at[p])

    weights = [
        [
            pltpu.make_async_copy(src.at[b], dst.at[b], w_sem.at[b, n])
            for n, (src, dst) in enumerate(
                ((wqkv_hbm, wqkv), (wout_hbm, wout), (wup_hbm, wup), (wdown_hbm, wdown))
            )
        ]
        for b in range(2)
    ]
    tok_copy(3).start()
    for n in range(4):
        weights[0][n].start()
    for p in range(3):
        tok_copy(p).start()
    for n in range(4):
        weights[1][n].start()

    up, down = lax.rem(lat + lats - 1, lats), lax.rem(lat + 1, lats)
    barrier = pltpu.get_barrier_semaphore()
    for partner in ((lat, left), (lat, right), (up, lon), (up, right), (down, lon), (down, left)):
        place = {"lat": partner[0], "lon": partner[1]}
        pl.semaphore_signal(barrier, inc=1, device_id=place, device_id_type=MESH)

    qkv[:, TOK:PAD, :] = jnp.zeros((10, PAD - TOK, 1536), BF)
    bias[...] = jnp.zeros((32, TOK, 256), F32)
    one = jnp.ones((1, 128), F32)
    vflag = flag_rows(valid_ref, None)

    @pl.when(south)
    def _():
        for w, (band, j) in enumerate(ORDER):
            if band == 1:
                bias[w] = window_bias([vflag[r : r + 1] for r in range(2, 8)], 12 * j)

    @pl.when(north)
    def _():
        for j in range(3):
            bias[8 + j] = window_bias([0.0 * one] * 3 + [one] * 3, 6 + 12 * j)
        bias[16] = window_bias([0.0 * one] * 3 + [one] * 3, 42)

    @pl.when(north)
    def _():
        ext[0:3] = jnp.zeros((3, 48, 512), BF)
        diag_in[...] = jnp.zeros((32, 512), BF)

    def send(src, dst, ssem, rsem, target):
        place = {"lat": target[0], "lon": target[1]}
        return pltpu.make_async_remote_copy(
            src_ref=src, dst_ref=dst, send_sem=ssem, recv_sem=rsem, device_id=place, device_id_type=MESH
        )

    v_copy = send(valid_ref.at[pl.ds(40, 8)], vhalo, v_s, v_r, (lat, left))

    def halo_copy(p):
        return send(halo_out.at[p], halo_in.at[p], halo_s.at[p], halo_r.at[p], (lat, left))

    row_copy = send(ext.at[pl.ds(48, 3)], ext.at[pl.ds(0, 3)], row_s, row_r, (lat + 1, lon))
    diag_copy = send(halo_out.at[3, pl.ds(48, 32)], diag_in, diag_s, diag_r, (lat + 1, left))

    def ret_copy(n):
        rows = pl.ds(144 * n, 144)
        return send(outgoing.at[rows], ret.at[rows], ret_s.at[n], ret_r.at[n], (lat, right))

    below_copy = send(yext.at[pl.ds(0, 3)], yext.at[pl.ds(48, 3)], below_s, below_r, (lat - 1, lon))
    corner_copy = send(outgoing.at[pl.ds(0, 32)], edge_in, corner_s, corner_r, (lat - 1, right))
    pole_copy = send(edge_out, edge_in, pole_s, corner_r, (lat, right))

    def out_copy(n, low, size):
        return pltpu.make_async_copy(
            yext.at[pl.ds(low, size)], out_hbm.at[pl.ds(low - 3, size)], out_sem.at[n]
        )

    sets = [sets_ref[i] for i in range(6)]

    def gather0(p):
        x = tok[pl.ds(12 * p, 12)].astype(F32)
        for w, (band, j) in enumerate(ORDER):
            wide[TOK * w : TOK * w + TOK] = jnp.concatenate(
                [x[6 * band + r, 12 * j : 12 * j + 12] for r in range(6)], 0
            )

    def gather_inner(p):
        x = ext[12 * p : 12 * p + 12].astype(F32)
        for w, (band, j) in enumerate(INNER):
            wide[TOK * w : TOK * w + TOK] = jnp.concatenate(
                [x[6 * band + r, 12 * j + 6 : 12 * j + 18] for r in range(6)], 0
            )

    def gather_right():
        x = ext[:, 32:48].astype(F32)
        came = [halo_in[n].astype(F32) for n in range(4)]
        above = diag_in[...].astype(F32)

        def row(at):
            if at < 3:
                other = above[6 + 6 * at : 12 + 6 * at]
            else:
                n, r = (at - 3) // 12, (at - 3) % 12
                other = came[n][6 * r : 6 * r + 6]
            return [x[at, 10:16], other]

        for band in range(8):
            wide[TOK * band : TOK * band + TOK] = jnp.concatenate(
                [part for r in range(6) for part in row(6 * band + r)], 0
            )
        edge = ext[48:51].astype(F32)
        half = [edge[r, 12 * j + 6 : 12 * j + 18] for j in range(3) for r in range(3)]
        wide[8 * TOK : 10 * TOK] = jnp.concatenate(half + [part for r in range(3) for part in row(48 + r)], 0)

    def project(b, x, tokens):
        out = jnp.dot(layer_norm(x), wqkv[b], preferred_element_type=F32)
        for w in range(tokens // TOK):
            qkv[w, 0:TOK, :] = out[TOK * w : TOK * w + TOK].astype(BF)

    def attend(pair, flagged):
        for g in range(2):
            both = []
            for w in (2 * pair, 2 * pair + 1):
                q = qkv[w, :, 256 * g : 256 * g + 256]
                k = qkv[w, :, 512 + 256 * g : 768 + 256 * g]
                v = qkv[w, :, 1024 + 256 * g : 1280 + 256 * g]
                both.append(half_heads(q, k, v, sets, None if flagged is None else bias[flagged + w, :, 0 : 3 * PAD]))
            mixed[2 * TOK * pair : 2 * TOK * pair + 2 * TOK, 256 * g : 256 * g + 256] = jnp.concatenate(
                both, 0
            ).astype(BF)

    def add_mixed(b, rows):
        total = wide[rows] + jnp.dot(mixed[rows], wout[b], preferred_element_type=F32)
        total = total.astype(BF)
        resid[rows] = total
        return layer_norm(total.astype(F32))

    def expand(b, normed, rows, n):
        cut = slice(512 * n, 512 * n + 512)
        hidden[rows, cut] = twice_gelu(jnp.dot(normed, wup[b, :, cut], preferred_element_type=F32)).astype(BF)

    def contract(b, rows):
        return resid[rows].astype(F32) + 0.5 * jnp.dot(hidden[rows], wdown[b], preferred_element_type=F32)

    def scatter0(y, p):
        rows = [
            y[TOK * w + 12 * r : TOK * w + 12 * r + 12]
            for band in range(2)
            for r in range(6)
            for w in (ORDER.index((band, j)) for j in range(4))
        ]
        ext[pl.ds(3 + 12 * p, 12)] = jnp.concatenate(rows, 0).astype(BF).reshape(12, 48, 512)
        part = [
            y[TOK * w + 12 * r : TOK * w + 12 * r + 6] for w in (ORDER.index((band, 0)) for band in range(2)) for r in range(6)
        ]
        halo_out[p] = jnp.concatenate(part + [jnp.zeros((PAD - TOK, 512), F32)], 0).astype(BF)

    def settle(y, p):
        gap = jnp.zeros((6, 512), F32)
        for band in range(2):
            for r in range(6):
                row = [y[TOK * w + 12 * r : TOK * w + 12 * r + 12] for w in range(3 * band, 3 * band + 3)]
                yext[12 * p + 6 * band + r] = jnp.concatenate([gap] + row + [gap], 0).astype(BF)

    def settle_right(y):
        starts = [TOK * band + 12 * r for band in range(8) for r in range(6)]
        inner[...] = jnp.concatenate([y[at : at + 6] for at in starts], 0).astype(BF)
        outgoing[...] = jnp.concatenate([y[at + 6 : at + 12] for at in starts], 0).astype(BF)

        @pl.when(south)
        def _():
            edge = y[8 * TOK : 10 * TOK]
            part = [edge[108 + 12 * r + 6 : 108 + 12 * r + 12] for r in range(3)]
            edge_out[...] = jnp.concatenate(part + [jnp.zeros((14, 512), F32)], 0).astype(BF)
            for r in range(3):
                row = [edge[36 * j + 12 * r : 36 * j + 12 * r + 12] for j in range(4)]
                yext[48 + r] = jnp.concatenate([jnp.zeros((6, 512), F32)] + row, 0)[0:48].astype(BF)

    def step(b_feed, feed_count, b_att, gather, att_count, finish, flagged=None):
        rows = slice(0, TOK * feed_count)
        normed = add_mixed(b_feed, rows)
        gather()
        project(b_att, wide[0 : TOK * att_count], TOK * att_count)
        for n in range(4):
            expand(b_feed, normed, rows, n)
            if n < att_count // 2:
                attend(n, flagged)
        for n in range(4, att_count // 2):
            attend(n, flagged)
        finish(contract(b_feed, rows))

    tok_copy(3).wait()
    weights[0][0].wait()
    gather0(3)
    project(0, wide[0:576], 576)
    for n in range(4):
        attend(n, 0)

    for n in range(1, 4):
        weights[0][n].wait()
    pl.semaphore_wait(barrier, 6)
    v_copy.start()

    def block0(p, carry):
        tok_copy(p).wait()
        before = lax.rem(p + 3, 4)
        step(0, 8, 0, lambda: gather0(p), 8, lambda y: scatter0(y, before))

        @pl.when((p == 0) & ~south)
        def _():
            row_copy.start()
            diag_copy.start()

        halo_copy(before).start()
        return carry

    lax.fori_loop(0, 3, block0, 0)

    v_copy.wait()
    vflag = flag_rows(valid_ref, vhalo)
    for n in range(4):
        weights[1][n].wait()

    @pl.when(south)
    def _():
        rows = [one] + [vflag[r : r + 1] for r in range(5)]
        bias[23] = window_bias(rows, 42)
        for j in range(3):
            bias[26 + 3 + j] = window_bias(rows, 6 + 12 * j)
        for w in range(2):
            bias[24 + w] = window_bias([vflag[r : r + 1] for r in range(5, 8)], 6 + 24 * w, halves=True)

    @pl.when(~north)
    def _():
        row_copy.wait_recv()

    step(0, 8, 1, lambda: gather_inner(0), 6, lambda y: scatter0(y, 2), flagged=8)
    halo_copy(2).start()

    step(1, 6, 1, lambda: gather_inner(1), 6, lambda y: settle(y, 0))

    @pl.when(~north)
    def _():
        diag_copy.wait_recv()

    for p in (3, 0, 1, 2):
        halo_copy(p).wait_recv()
    step(1, 6, 1, gather_right, 10, lambda y: settle(y, 1), flagged=16)
    step(1, 10, 1, lambda: gather_inner(2), 6, settle_right)
    for r in range(3):
        yext[r, 32:48] = jnp.concatenate(
            [yext[r, 32:42].astype(F32), inner[6 * r : 6 * r + 6].astype(F32)], 0
        ).astype(BF)
    ret_copy(0).start()
    ret_copy(1).start()

    @pl.when(~north)
    def _():
        below_copy.start()
        corner_copy.start()

    @pl.when(south)
    def _():
        pole_copy.start()

    step(1, 6, 1, lambda: gather_inner(3), 6, lambda y: settle(y, 2), flagged=26)

    def merge(low, high):
        came = ret[6 * low : 6 * high].astype(F32)
        mine = inner[6 * low : 6 * high].astype(F32)
        for r in range(high - low):
            own = yext[low + r, 0:HALO].astype(F32)
            yext[low + r, 0:HALO] = jnp.concatenate([came[6 * r : 6 * r + 6], own[6:]], 0).astype(BF)
            own = yext[low + r, 32:48].astype(F32)
            yext[low + r, 32:48] = jnp.concatenate([own[:10], mine[6 * r : 6 * r + 6]], 0).astype(BF)

    rows = slice(0, 6 * TOK)
    normed = add_mixed(1, rows)
    for n in range(4):
        expand(1, normed, rows, n)
    ret_copy(0).wait_recv()
    ret_copy(1).wait_recv()
    merge(3, 36)
    out_copy(0, 3, 9).start()
    out_copy(1, 12, 12).start()
    out_copy(2, 24, 12).start()
    settle(contract(1, rows), 3)
    merge(36, 48)

    @pl.when(~south)
    def _():
        below_copy.wait_recv()
        corner_copy.wait_recv()

    @pl.when(south)
    def _():
        pole_copy.wait()

    came = edge_in[...].astype(F32)
    for r in range(3):
        yext[48 + r, 0:HALO] = jnp.concatenate(
            [came[6 * r : 6 * r + 6], yext[48 + r, 0:HALO].astype(F32)[6:]], 0
        ).astype(BF)
    lane = lax.broadcasted_iota(jnp.int32, (48, 128), 1)
    sub = lax.broadcasted_iota(jnp.int32, (48, 128), 0)
    for r in range(8):
        keep = jnp.sum(jnp.where(lane == sub, vflag[r : r + 1], 0.0), axis=1, keepdims=True)
        yext[43 + r] = (yext[43 + r].astype(F32) * keep).astype(BF)
    out_copy(3, 36, 15).start()

    for p in range(4):
        halo_copy(p).wait_send()
    for n in range(2):
        ret_copy(n).wait_send()

    @pl.when(~south)
    def _():
        row_copy.wait_send()
        diag_copy.wait_send()

    @pl.when(~north)
    def _():
        below_copy.wait_send()
        corner_copy.wait_send()

    out_copy(0, 3, 9).wait()
    out_copy(1, 12, 12).wait()
    out_copy(2, 24, 12).wait()
    out_copy(3, 36, 15).wait()


def flag_rows(valid_ref, vhalo):
    parts = [valid_ref[40:48, :].astype(F32)]
    if vhalo is not None:
        parts += [vhalo[:, 0:HALO].astype(F32), jnp.zeros((8, 64), F32)]
    else:
        parts.append(jnp.zeros((8, 80), F32))
    return jnp.concatenate(parts, axis=1)


def deliver(src, dst, held, load_sem, store_sem):
    parts = [pl.ds(6 * n, 6) for n in range(8)]
    loads = [pltpu.make_async_copy(src.at[part], held.at[part], load_sem.at[n]) for n, part in enumerate(parts)]
    stores = [pltpu.make_async_copy(held.at[part], dst.at[part], store_sem.at[n]) for n, part in enumerate(parts)]
    for load in loads:
        load.start()
    for load, store in zip(loads, stores):
        load.wait()
        store.start()
    for store in stores:
        store.wait()


def shards(tokens, valid, w_qkv, w_out, w_up, w_down):
    vmem = pl.BlockSpec(memory_space=pltpu.VMEM)
    hbm = pl.BlockSpec(memory_space=pl.ANY)
    dma = pltpu.SemaphoreType.DMA
    result = jax.ShapeDtypeStruct((48, 48, 512), BF)
    done = pl.pallas_call(
        kernel,
        out_shape=result,
        in_specs=[hbm, vmem] + [hbm] * 4 + [vmem],
        out_specs=hbm,
        scratch_shapes=[
            pltpu.VMEM((48, 48, 512), BF),
            pltpu.VMEM((51, 48, 512), BF),
            pltpu.VMEM((51, 48, 512), BF),
            pltpu.VMEM((4, PAD, 512), BF),
            pltpu.VMEM((4, PAD, 512), BF),
            pltpu.VMEM((32, 512), BF),
            pltpu.VMEM((288, 512), BF),
            pltpu.VMEM((288, 512), BF),
            pltpu.VMEM((288, 512), BF),
            pltpu.VMEM((32, 512), BF),
            pltpu.VMEM((32, 512), BF),
            pltpu.VMEM((8, 48), jnp.int32),
            pltpu.VMEM((2, 512, 1536), BF),
            pltpu.VMEM((2, 512, 512), BF),
            pltpu.VMEM((2, 512, 2048), BF),
            pltpu.VMEM((2, 2048, 512), BF),
            pltpu.VMEM((10, PAD, 1536), BF),
            pltpu.VMEM((720, 512), BF),
            pltpu.VMEM((720, 512), F32),
            pltpu.VMEM((720, 512), BF),
            pltpu.VMEM((720, 2048), BF),
            pltpu.VMEM((32, TOK, 256), F32),
            dma((4,)), dma((2, 4)), dma((4,)),
            dma((4,)), dma((4,)), dma(()), dma(()), dma(()), dma(()), dma(()), dma(()),
            dma((2,)), dma((2,)), dma(()), dma(()), dma(()), dma(()), dma(()),
        ],
        compiler_params=pltpu.CompilerParams(
            collective_id=0, has_side_effects=True, vmem_limit_bytes=60 << 20
        ),
        name="swin",
    )(tokens, valid, w_qkv, w_out, w_up, w_down, jnp.asarray(head_sets(), BF))
    return pl.pallas_call(
        deliver,
        out_shape=result,
        in_specs=[hbm],
        out_specs=hbm,
        scratch_shapes=[pltpu.VMEM((48, 48, 512), BF), dma((8,)), dma((8,))],
        name="deliver",
    )(done)


def solution(mesh):
    return jax.shard_map(
        shards,
        mesh=mesh,
        in_specs=(P("lat", "lon", None), P("lat", "lon"), P(), P(), P(), P()),
        out_specs=P("lat", "lon", None),
        check_vma=False,
    )
```

```python
import jax
import jax.numpy as jnp
import numpy as np
from jax import lax
from jax.experimental import pallas as pl
from jax.experimental.pallas import tpu as pltpu
from jax.sharding import PartitionSpec as P

HEADS = 16
WIN_H = 6
WIN_W = 12
TOK = WIN_H * WIN_W
PAD = 80
HALO = 16
MESH = pl.DeviceIdType.MESH
BF = jnp.bfloat16
F32 = jnp.float32


ORDER = [(0, 0), (0, 1), (0, 2), (1, 0), (1, 1), (1, 2), (0, 3), (1, 3)]
INNER = ORDER[:6]
SCALE = 1.4426950408889634 * 32**-0.5


def head_sets():
    head = np.arange(256) // 32
    return np.stack([head // 3 == i for i in range(3)] + [head % 3 == j for j in range(3)])[:, None, :]


def layer_norm(wide):
    center = wide - jnp.mean(wide, axis=-1, keepdims=True)
    spread = jnp.mean(center * center, axis=-1, keepdims=True)
    return (center * lax.rsqrt(spread + 1e-05)).astype(BF)


def twice_gelu(x):
    return x + x * jnp.tanh(x * (0.7978845608028654 + 0.035677408136300125 * (x * x)))


def half_heads(q, k, v, sets, bias):
    by_key = jnp.concatenate([k * sets[i] for i in range(3)], 0)
    by_query = jnp.concatenate([q * sets[3 + j] for j in range(3)], 0)
    scores = lax.dot_general(by_key, by_query, (((1,), (1,)), ((), ())), preferred_element_type=F32)
    parts = []
    for i in range(3):
        part = scores[PAD * i : PAD * i + TOK]
        if bias is not None:
            part = part + bias
        largest = jnp.max(part, axis=0, keepdims=True)
        expo = jnp.exp2((part - largest) * SCALE)
        total = jnp.sum(expo, axis=0, keepdims=True)
        parts += [expo * (1.0 / total), jnp.zeros((PAD - TOK, 3 * PAD), F32)]
    probs = jnp.concatenate(parts, 0).astype(BF)
    by_value = jnp.concatenate([v * sets[i] for i in range(3)], 0)
    mixed = lax.dot_general(probs, by_value, (((0,), (0,)), ((), ())), preferred_element_type=F32)
    pick = [sets[3 + j].astype(F32) for j in range(3)]
    return (
        mixed[:TOK] * pick[0] + mixed[PAD : PAD + TOK] * pick[1] + mixed[2 * PAD : 2 * PAD + TOK] * pick[2]
    )


def window_bias(rows, first_col, halves=False):
    t = lax.broadcasted_iota(jnp.int32, (TOK, 128), 0)
    lane = lax.broadcasted_iota(jnp.int32, (TOK, 128), 1)
    tall = jnp.zeros((TOK, 128), F32)
    at = lane - first_col
    for half in range(2 if halves else 1):
        for r, row in enumerate(rows):
            low = (half * len(rows) + r) * WIN_W
            here = (t >= low) & (t < low + WIN_W) & (at == t - low + half * WIN_W)
            tall = jnp.where(here, row, tall)
    flag = jnp.sum(tall, axis=1, keepdims=True)
    key = lax.broadcasted_iota(jnp.int32, (TOK, 256), 0)
    query = lax.broadcasted_iota(jnp.int32, (TOK, 256), 1)
    query = query - PAD * ((query >= PAD).astype(jnp.int32) + (query >= 2 * PAD).astype(jnp.int32))
    allow = flag > 0.5
    if halves:
        allow = allow & ((key < TOK // 2) == (query < TOK // 2))
    allow = allow | (key == query) | (query >= TOK)
    return jnp.where(allow, 0.0, -jnp.inf)


def kernel(
    tok_hbm, valid_ref, wqkv_hbm, wout_hbm, wup_hbm, wdown_hbm, sets_ref,
    out_hbm,
    tok, ext, yext, halo_out, halo_in, diag_in, inner, outgoing, ret, edge_out, edge_in, turn_in, vhalo, wqkv, wout, wup, wdown, qkv, mixed, wide, resid, hidden, bias,
    tok_sem, w_sem, out_sem, halo_s, halo_r, row_s, row_r, diag_s, diag_r, v_s, v_r,
    ret_s, ret_r, corner_s, corner_r, pole_s, below_s, below_r, turn_s, turn_r,
):
    lat, lon = lax.axis_index("lat"), lax.axis_index("lon")
    lats, lons = lax.axis_size("lat"), lax.axis_size("lon")
    north, south = lat == 0, lat == lats - 1
    left, right = lax.rem(lon + lons - 1, lons), lax.rem(lon + 1, lons)

    def tok_copy(p):
        return pltpu.make_async_copy(tok_hbm.at[pl.ds(12 * p, 12)], tok.at[pl.ds(12 * p, 12)], tok_sem.at[p])

    weights = [
        [
            pltpu.make_async_copy(src.at[b], dst.at[b], w_sem.at[b, n])
            for n, (src, dst) in enumerate(
                ((wqkv_hbm, wqkv), (wout_hbm, wout), (wup_hbm, wup), (wdown_hbm, wdown))
            )
        ]
        for b in range(2)
    ]
    tok_copy(3).start()
    for n in range(4):
        weights[0][n].start()
    for p in range(3):
        tok_copy(p).start()
    for n in range(4):
        weights[1][n].start()

    up, down = lax.rem(lat + lats - 1, lats), lax.rem(lat + 1, lats)
    barrier = pltpu.get_barrier_semaphore()
    for partner in ((lat, left), (lat, right), (up, lon), (up, right), (down, lon), (down, left)):
        place = {"lat": partner[0], "lon": partner[1]}
        pl.semaphore_signal(barrier, inc=1, device_id=place, device_id_type=MESH)

    qkv[:, TOK:PAD, :] = jnp.zeros((10, PAD - TOK, 1536), BF)
    bias[...] = jnp.zeros((32, TOK, 256), F32)
    one = jnp.ones((1, 128), F32)
    vflag = flag_rows(valid_ref, None)

    @pl.when(south)
    def _():
        for w, (band, j) in enumerate(ORDER):
            if band == 1:
                bias[w] = window_bias([vflag[r : r + 1] for r in range(2, 8)], 12 * j)

    @pl.when(north)
    def _():
        for j in range(3):
            bias[8 + j] = window_bias([0.0 * one] * 3 + [one] * 3, 6 + 12 * j)
        bias[16] = window_bias([0.0 * one] * 3 + [one] * 3, 42)

    @pl.when(north)
    def _():
        ext[0:3] = jnp.zeros((3, 48, 512), BF)
        diag_in[...] = jnp.zeros((32, 512), BF)

    def send(src, dst, ssem, rsem, target):
        place = {"lat": target[0], "lon": target[1]}
        return pltpu.make_async_remote_copy(
            src_ref=src, dst_ref=dst, send_sem=ssem, recv_sem=rsem, device_id=place, device_id_type=MESH
        )

    v_copy = send(valid_ref.at[pl.ds(40, 8)], vhalo, v_s, v_r, (lat, left))

    def halo_copy(p):
        return send(halo_out.at[p], halo_in.at[p], halo_s.at[p], halo_r.at[p], (lat, left))

    row_copy = send(ext.at[pl.ds(48, 3)], ext.at[pl.ds(0, 3)], row_s, row_r, (lat + 1, lon))
    diag_copy = send(halo_out.at[3, pl.ds(48, 32)], diag_in, diag_s, diag_r, (lat + 1, left))

    def ret_copy(n):
        rows = pl.ds(144 * n, 144)
        return send(outgoing.at[rows], ret.at[rows], ret_s.at[n], ret_r.at[n], (lat, right))

    below_copy = send(yext.at[pl.ds(0, 3)], yext.at[pl.ds(48, 3)], below_s, below_r, (lat - 1, lon))
    turn_copy = send(inner.at[pl.ds(0, 32)], turn_in, turn_s, turn_r, (lat - 1, lon))
    corner_copy = send(outgoing.at[pl.ds(0, 32)], edge_in, corner_s, corner_r, (lat - 1, right))
    pole_copy = send(edge_out, edge_in, pole_s, corner_r, (lat, right))

    def out_copy(n, low, size):
        return pltpu.make_async_copy(
            yext.at[pl.ds(low, size)], out_hbm.at[pl.ds(low - 3, size)], out_sem.at[n]
        )

    sets = [sets_ref[i] for i in range(6)]

    def gather0(p):
        x = tok[pl.ds(12 * p, 12)].astype(F32)
        for w, (band, j) in enumerate(ORDER):
            wide[TOK * w : TOK * w + TOK] = jnp.concatenate(
                [x[6 * band + r, 12 * j : 12 * j + 12] for r in range(6)], 0
            )

    def gather_inner(p):
        x = ext[12 * p : 12 * p + 12].astype(F32)
        for w, (band, j) in enumerate(INNER):
            wide[TOK * w : TOK * w + TOK] = jnp.concatenate(
                [x[6 * band + r, 12 * j + 6 : 12 * j + 18] for r in range(6)], 0
            )

    def gather_right():
        x = ext[:, 32:48].astype(F32)
        came = [halo_in[n].astype(F32) for n in range(4)]
        above = diag_in[...].astype(F32)

        def row(at):
            if at < 3:
                other = above[6 + 6 * at : 12 + 6 * at]
            else:
                n, r = (at - 3) // 12, (at - 3) % 12
                other = came[n][6 * r : 6 * r + 6]
            return [x[at, 10:16], other]

        for band in range(8):
            wide[TOK * band : TOK * band + TOK] = jnp.concatenate(
                [part for r in range(6) for part in row(6 * band + r)], 0
            )
        edge = ext[48:51].astype(F32)
        half = [edge[r, 12 * j + 6 : 12 * j + 18] for j in range(3) for r in range(3)]
        wide[8 * TOK : 10 * TOK] = jnp.concatenate(half + [part for r in range(3) for part in row(48 + r)], 0)

    def project(b, x, tokens):
        out = jnp.dot(layer_norm(x), wqkv[b], preferred_element_type=F32)
        for w in range(tokens // TOK):
            qkv[w, 0:TOK, :] = out[TOK * w : TOK * w + TOK].astype(BF)

    def attend(pair, flagged):
        for g in range(2):
            both = []
            for w in (2 * pair, 2 * pair + 1):
                q = qkv[w, :, 256 * g : 256 * g + 256]
                k = qkv[w, :, 512 + 256 * g : 768 + 256 * g]
                v = qkv[w, :, 1024 + 256 * g : 1280 + 256 * g]
                both.append(half_heads(q, k, v, sets, None if flagged is None else bias[flagged + w, :, 0 : 3 * PAD]))
            mixed[2 * TOK * pair : 2 * TOK * pair + 2 * TOK, 256 * g : 256 * g + 256] = jnp.concatenate(
                both, 0
            ).astype(BF)

    def add_mixed(b, rows):
        total = wide[rows] + jnp.dot(mixed[rows], wout[b], preferred_element_type=F32)
        total = total.astype(BF)
        resid[rows] = total
        return layer_norm(total.astype(F32))

    def expand(b, normed, rows, n):
        cut = slice(512 * n, 512 * n + 512)
        hidden[rows, cut] = twice_gelu(jnp.dot(normed, wup[b, :, cut], preferred_element_type=F32)).astype(BF)

    def contract(b, rows):
        return resid[rows].astype(F32) + 0.5 * jnp.dot(hidden[rows], wdown[b], preferred_element_type=F32)

    def scatter0(y, p):
        rows = [
            y[TOK * w + 12 * r : TOK * w + 12 * r + 12]
            for band in range(2)
            for r in range(6)
            for w in (ORDER.index((band, j)) for j in range(4))
        ]
        ext[pl.ds(3 + 12 * p, 12)] = jnp.concatenate(rows, 0).astype(BF).reshape(12, 48, 512)
        part = [
            y[TOK * w + 12 * r : TOK * w + 12 * r + 6] for w in (ORDER.index((band, 0)) for band in range(2)) for r in range(6)
        ]
        halo_out[p] = jnp.concatenate(part + [jnp.zeros((PAD - TOK, 512), F32)], 0).astype(BF)

    def settle(y, p):
        gap = jnp.zeros((6, 512), F32)
        for band in range(2):
            for r in range(6):
                row = [y[TOK * w + 12 * r : TOK * w + 12 * r + 12] for w in range(3 * band, 3 * band + 3)]
                yext[12 * p + 6 * band + r] = jnp.concatenate([gap] + row + [gap], 0).astype(BF)

    def settle_right(y):
        starts = [TOK * band + 12 * r for band in range(8) for r in range(6)]
        inner[...] = jnp.concatenate([y[at : at + 6] for at in starts], 0).astype(BF)
        outgoing[...] = jnp.concatenate([y[at + 6 : at + 12] for at in starts], 0).astype(BF)

        @pl.when(south)
        def _():
            edge = y[8 * TOK : 10 * TOK]
            part = [edge[108 + 12 * r + 6 : 108 + 12 * r + 12] for r in range(3)]
            edge_out[...] = jnp.concatenate(part + [jnp.zeros((14, 512), F32)], 0).astype(BF)
            for r in range(3):
                row = [edge[36 * j + 12 * r : 36 * j + 12 * r + 12] for j in range(4)]
                yext[48 + r] = jnp.concatenate([jnp.zeros((6, 512), F32)] + row, 0)[0:48].astype(BF)

    def step(b_feed, feed_count, b_att, gather, att_count, finish, flagged=None):
        rows = slice(0, TOK * feed_count)
        normed = add_mixed(b_feed, rows)
        gather()
        project(b_att, wide[0 : TOK * att_count], TOK * att_count)
        pairs = att_count // 2
        for n in range(4):
            expand(b_feed, normed, rows, n)
            if n < pairs - 1:
                attend(n, flagged)
        y = contract(b_feed, rows)
        for n in range(min(4, pairs - 1), pairs):
            attend(n, flagged)
        finish(y)

    tok_copy(3).wait()
    weights[0][0].wait()
    gather0(3)
    project(0, wide[0:576], 576)
    for n in range(4):
        attend(n, 0)

    for n in range(1, 4):
        weights[0][n].wait()
    pl.semaphore_wait(barrier, 6)
    v_copy.start()

    def block0(p, carry):
        tok_copy(p).wait()
        before = lax.rem(p + 3, 4)
        step(0, 8, 0, lambda: gather0(p), 8, lambda y: scatter0(y, before))

        @pl.when((p == 0) & ~south)
        def _():
            row_copy.start()
            diag_copy.start()

        halo_copy(before).start()
        return carry

    lax.fori_loop(0, 3, block0, 0)

    v_copy.wait()
    vflag = flag_rows(valid_ref, vhalo)
    for n in range(4):
        weights[1][n].wait()

    @pl.when(south)
    def _():
        rows = [one] + [vflag[r : r + 1] for r in range(5)]
        bias[23] = window_bias(rows, 42)
        for j in range(3):
            bias[26 + 3 + j] = window_bias(rows, 6 + 12 * j)
        for w in range(2):
            bias[24 + w] = window_bias([vflag[r : r + 1] for r in range(5, 8)], 6 + 24 * w, halves=True)

    @pl.when(~north)
    def _():
        row_copy.wait_recv()

    step(0, 8, 1, lambda: gather_inner(0), 6, lambda y: scatter0(y, 2), flagged=8)
    halo_copy(2).start()

    step(1, 6, 1, lambda: gather_inner(1), 6, lambda y: settle(y, 0))

    @pl.when(~north)
    def _():
        below_copy.start()
        diag_copy.wait_recv()

    for p in (3, 0, 1, 2):
        halo_copy(p).wait_recv()
    step(1, 6, 1, gather_right, 10, lambda y: settle(y, 1), flagged=16)
    step(1, 10, 1, lambda: gather_inner(2), 6, settle_right)
    @pl.when(~north)
    def _():
        corner_copy.start()
        turn_copy.start()

    @pl.when(south)
    def _():
        pole_copy.start()

    ret_copy(0).start()
    ret_copy(1).start()

    step(1, 6, 1, lambda: gather_inner(3), 6, lambda y: settle(y, 2), flagged=26)

    def merge(low, high):
        came = ret[6 * low : 6 * high].astype(F32)
        mine = inner[6 * low : 6 * high].astype(F32)
        for r in range(high - low):
            own = yext[low + r, 0:HALO].astype(F32)
            yext[low + r, 0:HALO] = jnp.concatenate([came[6 * r : 6 * r + 6], own[6:]], 0).astype(BF)
            own = yext[low + r, 32:48].astype(F32)
            yext[low + r, 32:48] = jnp.concatenate([own[:10], mine[6 * r : 6 * r + 6]], 0).astype(BF)

    rows = slice(0, 6 * TOK)
    normed = add_mixed(1, rows)
    for n in range(4):
        expand(1, normed, rows, n)
    ret_copy(0).wait_recv()
    merge(3, 24)
    out_copy(0, 3, 9).start()
    out_copy(1, 12, 12).start()
    settle(contract(1, rows), 3)
    ret_copy(1).wait_recv()
    merge(24, 36)
    out_copy(2, 24, 12).start()
    merge(36, 48)

    @pl.when(~south)
    def _():
        below_copy.wait_recv()
        turn_copy.wait_recv()
        came = turn_in[...].astype(F32)
        for r in range(3):
            yext[48 + r, 32:48] = jnp.concatenate(
                [yext[48 + r, 32:48].astype(F32)[:10], came[6 * r : 6 * r + 6]], 0
            ).astype(BF)
        corner_copy.wait_recv()

    @pl.when(south)
    def _():
        pole_copy.wait()

    came = edge_in[...].astype(F32)
    for r in range(3):
        yext[48 + r, 0:HALO] = jnp.concatenate(
            [came[6 * r : 6 * r + 6], yext[48 + r, 0:HALO].astype(F32)[6:]], 0
        ).astype(BF)
    lane = lax.broadcasted_iota(jnp.int32, (48, 128), 1)
    sub = lax.broadcasted_iota(jnp.int32, (48, 128), 0)
    for r in range(8):
        keep = jnp.sum(jnp.where(lane == sub, vflag[r : r + 1], 0.0), axis=1, keepdims=True)
        yext[43 + r] = (yext[43 + r].astype(F32) * keep).astype(BF)
    out_copy(3, 36, 15).start()

    for p in range(4):
        halo_copy(p).wait_send()
    for n in range(2):
        ret_copy(n).wait_send()

    @pl.when(~south)
    def _():
        row_copy.wait_send()
        diag_copy.wait_send()

    @pl.when(~north)
    def _():
        below_copy.wait_send()
        turn_copy.wait_send()
        corner_copy.wait_send()

    out_copy(0, 3, 9).wait()
    out_copy(1, 12, 12).wait()
    out_copy(2, 24, 12).wait()
    out_copy(3, 36, 15).wait()


def flag_rows(valid_ref, vhalo):
    parts = [valid_ref[40:48, :].astype(F32)]
    if vhalo is not None:
        parts += [vhalo[:, 0:HALO].astype(F32), jnp.zeros((8, 64), F32)]
    else:
        parts.append(jnp.zeros((8, 80), F32))
    return jnp.concatenate(parts, axis=1)


def deliver(src, dst, held, load_sem, store_sem):
    parts = [pl.ds(6 * n, 6) for n in range(8)]
    loads = [pltpu.make_async_copy(src.at[part], held.at[part], load_sem.at[n]) for n, part in enumerate(parts)]
    stores = [pltpu.make_async_copy(held.at[part], dst.at[part], store_sem.at[n]) for n, part in enumerate(parts)]
    for load in loads:
        load.start()
    for load, store in zip(loads, stores):
        load.wait()
        store.start()
    for store in stores:
        store.wait()


def shards(tokens, valid, w_qkv, w_out, w_up, w_down):
    vmem = pl.BlockSpec(memory_space=pltpu.VMEM)
    hbm = pl.BlockSpec(memory_space=pl.ANY)
    dma = pltpu.SemaphoreType.DMA
    result = jax.ShapeDtypeStruct((48, 48, 512), BF)
    done = pl.pallas_call(
        kernel,
        out_shape=result,
        in_specs=[hbm, vmem] + [hbm] * 4 + [vmem],
        out_specs=hbm,
        scratch_shapes=[
            pltpu.VMEM((48, 48, 512), BF),
            pltpu.VMEM((51, 48, 512), BF),
            pltpu.VMEM((51, 48, 512), BF),
            pltpu.VMEM((4, PAD, 512), BF),
            pltpu.VMEM((4, PAD, 512), BF),
            pltpu.VMEM((32, 512), BF),
            pltpu.VMEM((288, 512), BF),
            pltpu.VMEM((288, 512), BF),
            pltpu.VMEM((288, 512), BF),
            pltpu.VMEM((32, 512), BF),
            pltpu.VMEM((32, 512), BF),
            pltpu.VMEM((32, 512), BF),
            pltpu.VMEM((8, 48), jnp.int32),
            pltpu.VMEM((2, 512, 1536), BF),
            pltpu.VMEM((2, 512, 512), BF),
            pltpu.VMEM((2, 512, 2048), BF),
            pltpu.VMEM((2, 2048, 512), BF),
            pltpu.VMEM((10, PAD, 1536), BF),
            pltpu.VMEM((720, 512), BF),
            pltpu.VMEM((720, 512), F32),
            pltpu.VMEM((720, 512), BF),
            pltpu.VMEM((720, 2048), BF),
            pltpu.VMEM((32, TOK, 256), F32),
            dma((4,)), dma((2, 4)), dma((4,)),
            dma((4,)), dma((4,)), dma(()), dma(()), dma(()), dma(()), dma(()), dma(()),
            dma((2,)), dma((2,)), dma(()), dma(()), dma(()), dma(()), dma(()), dma(()), dma(()),
        ],
        compiler_params=pltpu.CompilerParams(
            collective_id=0, has_side_effects=True, vmem_limit_bytes=60 << 20
        ),
        name="swin",
    )(tokens, valid, w_qkv, w_out, w_up, w_down, jnp.asarray(head_sets(), BF))
    return pl.pallas_call(
        deliver,
        out_shape=result,
        in_specs=[hbm],
        out_specs=hbm,
        scratch_shapes=[pltpu.VMEM((48, 48, 512), BF), dma((8,)), dma((8,))],
        name="deliver",
    )(done)


def solution(mesh):
    return jax.shard_map(
        shards,
        mesh=mesh,
        in_specs=(P("lat", "lon", None), P("lat", "lon"), P(), P(), P(), P()),
        out_specs=P("lat", "lon", None),
        check_vma=False,
    )
```

```python
import jax
import jax.numpy as jnp
import numpy as np
from jax import lax
from jax.experimental import pallas as pl
from jax.experimental.pallas import tpu as pltpu
from jax.sharding import PartitionSpec as P

HEADS = 16
WIN_H = 6
WIN_W = 12
TOK = WIN_H * WIN_W
PAD = 80
HALO = 16
MESH = pl.DeviceIdType.MESH
BF = jnp.bfloat16
F32 = jnp.float32


ORDER = [(0, 0), (0, 1), (0, 2), (1, 0), (1, 1), (1, 2), (0, 3), (1, 3)]
INNER = ORDER[:6]
SCALE = 1.4426950408889634 * 32**-0.5


def head_sets():
    head = np.arange(256) // 32
    return np.stack([head // 3 == i for i in range(3)] + [head % 3 == j for j in range(3)])[:, None, :]


def layer_norm(wide):
    center = wide - jnp.mean(wide, axis=-1, keepdims=True)
    spread = jnp.mean(center * center, axis=-1, keepdims=True)
    return (center * lax.rsqrt(spread + 1e-05)).astype(BF)


def twice_gelu(x):
    return x + x * jnp.tanh(x * (0.7978845608028654 + 0.035677408136300125 * (x * x)))


def half_heads(q, k, v, sets, bias):
    by_key = jnp.concatenate([k * sets[i] for i in range(3)], 0)
    by_query = jnp.concatenate([q * sets[3 + j] for j in range(3)], 0)
    scores = lax.dot_general(by_key, by_query, (((1,), (1,)), ((), ())), preferred_element_type=F32)
    parts = []
    for i in range(3):
        part = scores[PAD * i : PAD * i + TOK]
        if bias is not None:
            part = part + bias
        largest = jnp.max(part, axis=0, keepdims=True)
        expo = jnp.exp2((part - largest) * SCALE)
        total = jnp.sum(expo, axis=0, keepdims=True)
        parts += [expo * (1.0 / total), jnp.zeros((PAD - TOK, 3 * PAD), F32)]
    probs = jnp.concatenate(parts, 0).astype(BF)
    by_value = jnp.concatenate([v * sets[i] for i in range(3)], 0)
    mixed = lax.dot_general(probs, by_value, (((0,), (0,)), ((), ())), preferred_element_type=F32)
    pick = [sets[3 + j].astype(F32) for j in range(3)]
    return (
        mixed[:TOK] * pick[0] + mixed[PAD : PAD + TOK] * pick[1] + mixed[2 * PAD : 2 * PAD + TOK] * pick[2]
    )


def window_bias(rows, first_col, halves=False):
    t = lax.broadcasted_iota(jnp.int32, (TOK, 128), 0)
    lane = lax.broadcasted_iota(jnp.int32, (TOK, 128), 1)
    tall = jnp.zeros((TOK, 128), F32)
    at = lane - first_col
    for half in range(2 if halves else 1):
        for r, row in enumerate(rows):
            low = (half * len(rows) + r) * WIN_W
            here = (t >= low) & (t < low + WIN_W) & (at == t - low + half * WIN_W)
            tall = jnp.where(here, row, tall)
    flag = jnp.sum(tall, axis=1, keepdims=True)
    key = lax.broadcasted_iota(jnp.int32, (TOK, 256), 0)
    query = lax.broadcasted_iota(jnp.int32, (TOK, 256), 1)
    query = query - PAD * ((query >= PAD).astype(jnp.int32) + (query >= 2 * PAD).astype(jnp.int32))
    allow = flag > 0.5
    if halves:
        allow = allow & ((key < TOK // 2) == (query < TOK // 2))
    allow = allow | (key == query) | (query >= TOK)
    return jnp.where(allow, 0.0, -jnp.inf)


def kernel(
    tok_hbm, valid_ref, wqkv_hbm, wout_hbm, wup_hbm, wdown_hbm, sets_ref,
    out_hbm,
    tok, ext, yext, halo_out, halo_in, diag_in, inner, outgoing, ret, edge_out, edge_in, turn_in, vhalo, wqkv, wout, wup, wdown, qkv, mixed, wide, resid, hidden, bias,
    tok_sem, w_sem, out_sem, halo_s, halo_r, row_s, row_r, diag_s, diag_r, v_s, v_r,
    ret_s, ret_r, corner_s, corner_r, pole_s, below_s, below_r, turn_s, turn_r,
):
    lat, lon = lax.axis_index("lat"), lax.axis_index("lon")
    lats, lons = lax.axis_size("lat"), lax.axis_size("lon")
    north, south = lat == 0, lat == lats - 1
    left, right = lax.rem(lon + lons - 1, lons), lax.rem(lon + 1, lons)

    def tok_copy(p):
        return pltpu.make_async_copy(tok_hbm.at[pl.ds(12 * p, 12)], tok.at[pl.ds(12 * p, 12)], tok_sem.at[p])

    weights = [
        [
            pltpu.make_async_copy(src.at[b], dst.at[b], w_sem.at[b, n])
            for n, (src, dst) in enumerate(
                ((wqkv_hbm, wqkv), (wout_hbm, wout), (wup_hbm, wup), (wdown_hbm, wdown))
            )
        ]
        for b in range(2)
    ]
    tok_copy(3).start()
    for n in range(4):
        weights[0][n].start()
    for p in range(3):
        tok_copy(p).start()
    for n in range(4):
        weights[1][n].start()

    up, down = lax.rem(lat + lats - 1, lats), lax.rem(lat + 1, lats)
    barrier = pltpu.get_barrier_semaphore()
    for partner in ((lat, left), (lat, right), (up, lon), (up, right), (down, lon), (down, left)):
        place = {"lat": partner[0], "lon": partner[1]}
        pl.semaphore_signal(barrier, inc=1, device_id=place, device_id_type=MESH)

    qkv[:, TOK:PAD, :] = jnp.zeros((10, PAD - TOK, 1536), BF)
    bias[...] = jnp.zeros((38, TOK, 256), F32)
    one = jnp.ones((1, 128), F32)
    vflag = flag_rows(valid_ref, None)

    @pl.when(south)
    def _():
        for w, (band, j) in enumerate(ORDER):
            if band == 1:
                bias[w] = window_bias([vflag[r : r + 1] for r in range(2, 8)], 12 * j)

    @pl.when(north)
    def _():
        for j in range(3):
            bias[8 + j] = window_bias([0.0 * one] * 3 + [one] * 3, 6 + 12 * j)
        bias[16] = window_bias([0.0 * one] * 3 + [one] * 3, 42)

    @pl.when(north)
    def _():
        ext[0:3] = jnp.zeros((3, 48, 512), BF)
        diag_in[...] = jnp.zeros((32, 512), BF)

    def send(src, dst, ssem, rsem, target):
        place = {"lat": target[0], "lon": target[1]}
        return pltpu.make_async_remote_copy(
            src_ref=src, dst_ref=dst, send_sem=ssem, recv_sem=rsem, device_id=place, device_id_type=MESH
        )

    v_copy = send(valid_ref.at[pl.ds(40, 8)], vhalo, v_s, v_r, (lat, left))

    def halo_copy(p):
        return send(halo_out.at[p], halo_in.at[p], halo_s.at[p], halo_r.at[p], (lat, left))

    row_copy = send(ext.at[pl.ds(48, 3)], ext.at[pl.ds(0, 3)], row_s, row_r, (lat + 1, lon))
    diag_copy = send(halo_out.at[3, pl.ds(48, 32)], diag_in, diag_s, diag_r, (lat + 1, left))

    def ret_copy(n):
        rows = pl.ds(144 * n, 144)
        return send(outgoing.at[rows], ret.at[rows], ret_s.at[n], ret_r.at[n], (lat, right))

    below_copy = send(yext.at[pl.ds(0, 3)], yext.at[pl.ds(48, 3)], below_s, below_r, (lat - 1, lon))
    turn_copy = send(inner.at[pl.ds(0, 32)], turn_in, turn_s, turn_r, (lat - 1, lon))
    corner_copy = send(outgoing.at[pl.ds(0, 32)], edge_in, corner_s, corner_r, (lat - 1, right))
    pole_copy = send(edge_out, edge_in, pole_s, corner_r, (lat, right))

    def out_copy(n, low, size):
        return pltpu.make_async_copy(
            yext.at[pl.ds(low, size)], out_hbm.at[pl.ds(low - 3, size)], out_sem.at[n]
        )

    sets = [sets_ref[i] for i in range(6)]

    def gather0(p):
        x = tok[pl.ds(12 * p, 12)].astype(F32)
        for w, (band, j) in enumerate(ORDER):
            wide[TOK * w : TOK * w + TOK] = jnp.concatenate(
                [x[6 * band + r, 12 * j : 12 * j + 12] for r in range(6)], 0
            )

    def gather_inner(p):
        x = ext[pl.ds(12 * p, 12)].astype(F32)
        for w, (band, j) in enumerate(INNER):
            wide[TOK * w : TOK * w + TOK] = jnp.concatenate(
                [x[6 * band + r, 12 * j + 6 : 12 * j + 18] for r in range(6)], 0
            )

    def gather_right():
        x = ext[:, 32:48].astype(F32)
        came = [halo_in[n].astype(F32) for n in range(4)]
        above = diag_in[...].astype(F32)

        def row(at):
            if at < 3:
                other = above[6 + 6 * at : 12 + 6 * at]
            else:
                n, r = (at - 3) // 12, (at - 3) % 12
                other = came[n][6 * r : 6 * r + 6]
            return [x[at, 10:16], other]

        for band in range(8):
            wide[TOK * band : TOK * band + TOK] = jnp.concatenate(
                [part for r in range(6) for part in row(6 * band + r)], 0
            )
        edge = ext[48:51].astype(F32)
        half = [edge[r, 12 * j + 6 : 12 * j + 18] for j in range(3) for r in range(3)]
        wide[8 * TOK : 10 * TOK] = jnp.concatenate(half + [part for r in range(3) for part in row(48 + r)], 0)

    def project(b, x, tokens):
        out = jnp.dot(layer_norm(x), wqkv[b], preferred_element_type=F32)
        for w in range(tokens // TOK):
            qkv[w, 0:TOK, :] = out[TOK * w : TOK * w + TOK].astype(BF)

    def attend(pair, flagged):
        for g in range(2):
            both = []
            for w in (2 * pair, 2 * pair + 1):
                q = qkv[w, :, 256 * g : 256 * g + 256]
                k = qkv[w, :, 512 + 256 * g : 768 + 256 * g]
                v = qkv[w, :, 1024 + 256 * g : 1280 + 256 * g]
                both.append(half_heads(q, k, v, sets, None if flagged is None else bias[flagged + w, :, 0 : 3 * PAD]))
            mixed[2 * TOK * pair : 2 * TOK * pair + 2 * TOK, 256 * g : 256 * g + 256] = jnp.concatenate(
                both, 0
            ).astype(BF)

    def add_mixed(b, rows):
        total = wide[rows] + jnp.dot(mixed[rows], wout[b], preferred_element_type=F32)
        total = total.astype(BF)
        resid[rows] = total
        return layer_norm(total.astype(F32))

    def expand(b, normed, rows, n):
        cut = slice(512 * n, 512 * n + 512)
        hidden[rows, cut] = twice_gelu(jnp.dot(normed, wup[b, :, cut], preferred_element_type=F32)).astype(BF)

    def contract(b, rows):
        return resid[rows].astype(F32) + 0.5 * jnp.dot(hidden[rows], wdown[b], preferred_element_type=F32)

    def scatter0(y, p):
        rows = [
            y[TOK * w + 12 * r : TOK * w + 12 * r + 12]
            for band in range(2)
            for r in range(6)
            for w in (ORDER.index((band, j)) for j in range(4))
        ]
        ext[pl.ds(3 + 12 * p, 12)] = jnp.concatenate(rows, 0).astype(BF).reshape(12, 48, 512)
        part = [
            y[TOK * w + 12 * r : TOK * w + 12 * r + 6] for w in (ORDER.index((band, 0)) for band in range(2)) for r in range(6)
        ]
        halo_out[p] = jnp.concatenate(part + [jnp.zeros((PAD - TOK, 512), F32)], 0).astype(BF)

    def settle(y, p):
        gap = jnp.zeros((6, 512), F32)
        for band in range(2):
            for r in range(6):
                row = [y[TOK * w + 12 * r : TOK * w + 12 * r + 12] for w in range(3 * band, 3 * band + 3)]
                yext[12 * p + 6 * band + r] = jnp.concatenate([gap] + row + [gap], 0).astype(BF)

    def settle_right(y):
        starts = [TOK * band + 12 * r for band in range(8) for r in range(6)]
        inner[...] = jnp.concatenate([y[at : at + 6] for at in starts], 0).astype(BF)
        outgoing[...] = jnp.concatenate([y[at + 6 : at + 12] for at in starts], 0).astype(BF)

        @pl.when(south)
        def _():
            edge = y[8 * TOK : 10 * TOK]
            part = [edge[108 + 12 * r + 6 : 108 + 12 * r + 12] for r in range(3)]
            edge_out[...] = jnp.concatenate(part + [jnp.zeros((14, 512), F32)], 0).astype(BF)
            for r in range(3):
                row = [edge[36 * j + 12 * r : 36 * j + 12 * r + 12] for j in range(4)]
                yext[48 + r] = jnp.concatenate([jnp.zeros((6, 512), F32)] + row, 0)[0:48].astype(BF)

    def step(b_feed, feed_count, b_att, gather, att_count, finish, flagged=None):
        rows = slice(0, TOK * feed_count)
        normed = add_mixed(b_feed, rows)
        gather()
        project(b_att, wide[0 : TOK * att_count], TOK * att_count)
        pairs = att_count // 2
        for n in range(4):
            expand(b_feed, normed, rows, n)
            if n < pairs - 1:
                attend(n, flagged)
        y = contract(b_feed, rows)
        for n in range(min(4, pairs - 1), pairs):
            attend(n, flagged)
        finish(y)

    tok_copy(3).wait()
    weights[0][0].wait()
    gather0(3)
    project(0, wide[0:576], 576)
    for n in range(4):
        attend(n, 0)

    for n in range(1, 4):
        weights[0][n].wait()
    pl.semaphore_wait(barrier, 6)
    v_copy.start()

    def block0(p, carry):
        tok_copy(p).wait()
        before = lax.rem(p + 3, 4)
        step(0, 8, 0, lambda: gather0(p), 8, lambda y: scatter0(y, before))

        @pl.when((p == 0) & ~south)
        def _():
            row_copy.start()
            diag_copy.start()

        halo_copy(before).start()
        return carry

    lax.fori_loop(0, 3, block0, 0)

    v_copy.wait()
    vflag = flag_rows(valid_ref, vhalo)
    for n in range(4):
        weights[1][n].wait()

    @pl.when(south)
    def _():
        rows = [one] + [vflag[r : r + 1] for r in range(5)]
        bias[23] = window_bias(rows, 42)
        for j in range(3):
            bias[35 + j] = window_bias(rows, 6 + 12 * j)
        for w in range(2):
            bias[24 + w] = window_bias([vflag[r : r + 1] for r in range(5, 8)], 6 + 24 * w, halves=True)

    @pl.when(~north)
    def _():
        row_copy.wait_recv()

    step(0, 8, 1, lambda: gather_inner(0), 6, lambda y: scatter0(y, 2), flagged=8)
    halo_copy(2).start()

    def block1(n, carry):
        p = 1 + 2 * n
        step(1, 6, 1, lambda: gather_inner(p), 6, lambda y: settle(y, p - 1), flagged=26 + 6 * n)

        @pl.when(n == 0)
        def _():
            @pl.when(~north)
            def _():
                below_copy.start()
                diag_copy.wait_recv()

            for k in (3, 0, 1, 2):
                halo_copy(k).wait_recv()
            step(1, 6, 1, gather_right, 10, lambda y: settle(y, 1), flagged=16)
            step(1, 10, 1, lambda: gather_inner(2), 6, settle_right)

            @pl.when(~north)
            def _():
                corner_copy.start()
                turn_copy.start()

            @pl.when(south)
            def _():
                pole_copy.start()

            ret_copy(0).start()
            ret_copy(1).start()

        return carry

    lax.fori_loop(0, 2, block1, 0)

    def merge(low, high):
        came = ret[6 * low : 6 * high].astype(F32)
        mine = inner[6 * low : 6 * high].astype(F32)
        for r in range(high - low):
            own = yext[low + r, 0:HALO].astype(F32)
            yext[low + r, 0:HALO] = jnp.concatenate([came[6 * r : 6 * r + 6], own[6:]], 0).astype(BF)
            own = yext[low + r, 32:48].astype(F32)
            yext[low + r, 32:48] = jnp.concatenate([own[:10], mine[6 * r : 6 * r + 6]], 0).astype(BF)

    rows = slice(0, 6 * TOK)
    normed = add_mixed(1, rows)
    for n in range(4):
        expand(1, normed, rows, n)
    ret_copy(0).wait_recv()
    merge(3, 24)
    out_copy(0, 3, 9).start()
    out_copy(1, 12, 12).start()
    settle(contract(1, rows), 3)
    ret_copy(1).wait_recv()
    merge(24, 36)
    out_copy(2, 24, 12).start()
    merge(36, 48)

    @pl.when(~south)
    def _():
        below_copy.wait_recv()
        turn_copy.wait_recv()
        came = turn_in[...].astype(F32)
        for r in range(3):
            yext[48 + r, 32:48] = jnp.concatenate(
                [yext[48 + r, 32:48].astype(F32)[:10], came[6 * r : 6 * r + 6]], 0
            ).astype(BF)
        corner_copy.wait_recv()

    @pl.when(south)
    def _():
        pole_copy.wait()

    came = edge_in[...].astype(F32)
    for r in range(3):
        yext[48 + r, 0:HALO] = jnp.concatenate(
            [came[6 * r : 6 * r + 6], yext[48 + r, 0:HALO].astype(F32)[6:]], 0
        ).astype(BF)
    lane = lax.broadcasted_iota(jnp.int32, (48, 128), 1)
    sub = lax.broadcasted_iota(jnp.int32, (48, 128), 0)
    for r in range(8):
        keep = jnp.sum(jnp.where(lane == sub, vflag[r : r + 1], 0.0), axis=1, keepdims=True)
        yext[43 + r] = (yext[43 + r].astype(F32) * keep).astype(BF)
    out_copy(3, 36, 15).start()

    for p in range(4):
        halo_copy(p).wait_send()
    for n in range(2):
        ret_copy(n).wait_send()

    @pl.when(~south)
    def _():
        row_copy.wait_send()
        diag_copy.wait_send()

    @pl.when(~north)
    def _():
        below_copy.wait_send()
        turn_copy.wait_send()
        corner_copy.wait_send()

    out_copy(0, 3, 9).wait()
    out_copy(1, 12, 12).wait()
    out_copy(2, 24, 12).wait()
    out_copy(3, 36, 15).wait()


def flag_rows(valid_ref, vhalo):
    parts = [valid_ref[40:48, :].astype(F32)]
    if vhalo is not None:
        parts += [vhalo[:, 0:HALO].astype(F32), jnp.zeros((8, 64), F32)]
    else:
        parts.append(jnp.zeros((8, 80), F32))
    return jnp.concatenate(parts, axis=1)


def deliver(src, dst, held, load_sem, store_sem):
    parts = [pl.ds(6 * n, 6) for n in range(8)]
    loads = [pltpu.make_async_copy(src.at[part], held.at[part], load_sem.at[n]) for n, part in enumerate(parts)]
    stores = [pltpu.make_async_copy(held.at[part], dst.at[part], store_sem.at[n]) for n, part in enumerate(parts)]
    for load in loads:
        load.start()
    for load, store in zip(loads, stores):
        load.wait()
        store.start()
    for store in stores:
        store.wait()


def shards(tokens, valid, w_qkv, w_out, w_up, w_down):
    vmem = pl.BlockSpec(memory_space=pltpu.VMEM)
    hbm = pl.BlockSpec(memory_space=pl.ANY)
    dma = pltpu.SemaphoreType.DMA
    result = jax.ShapeDtypeStruct((48, 48, 512), BF)
    done = pl.pallas_call(
        kernel,
        out_shape=result,
        in_specs=[hbm, vmem] + [hbm] * 4 + [vmem],
        out_specs=hbm,
        scratch_shapes=[
            pltpu.VMEM((48, 48, 512), BF),
            pltpu.VMEM((51, 48, 512), BF),
            pltpu.VMEM((51, 48, 512), BF),
            pltpu.VMEM((4, PAD, 512), BF),
            pltpu.VMEM((4, PAD, 512), BF),
            pltpu.VMEM((32, 512), BF),
            pltpu.VMEM((288, 512), BF),
            pltpu.VMEM((288, 512), BF),
            pltpu.VMEM((288, 512), BF),
            pltpu.VMEM((32, 512), BF),
            pltpu.VMEM((32, 512), BF),
            pltpu.VMEM((32, 512), BF),
            pltpu.VMEM((8, 48), jnp.int32),
            pltpu.VMEM((2, 512, 1536), BF),
            pltpu.VMEM((2, 512, 512), BF),
            pltpu.VMEM((2, 512, 2048), BF),
            pltpu.VMEM((2, 2048, 512), BF),
            pltpu.VMEM((10, PAD, 1536), BF),
            pltpu.VMEM((720, 512), BF),
            pltpu.VMEM((720, 512), F32),
            pltpu.VMEM((720, 512), BF),
            pltpu.VMEM((720, 2048), BF),
            pltpu.VMEM((38, TOK, 256), F32),
            dma((4,)), dma((2, 4)), dma((4,)),
            dma((4,)), dma((4,)), dma(()), dma(()), dma(()), dma(()), dma(()), dma(()),
            dma((2,)), dma((2,)), dma(()), dma(()), dma(()), dma(()), dma(()), dma(()), dma(()),
        ],
        compiler_params=pltpu.CompilerParams(
            collective_id=0, has_side_effects=True, vmem_limit_bytes=60 << 20
        ),
        name="swin",
    )(tokens, valid, w_qkv, w_out, w_up, w_down, jnp.asarray(head_sets(), BF))
    return pl.pallas_call(
        deliver,
        out_shape=result,
        in_specs=[hbm],
        out_specs=hbm,
        scratch_shapes=[pltpu.VMEM((48, 48, 512), BF), dma((8,)), dma((8,))],
        name="deliver",
    )(done)


def solution(mesh):
    return jax.shard_map(
        shards,
        mesh=mesh,
        in_specs=(P("lat", "lon", None), P("lat", "lon"), P(), P(), P(), P()),
        out_specs=P("lat", "lon", None),
        check_vma=False,
    )
```
